32 devices in a mesh: groups: 2 (over x), ctx: 16 (over z, y, core).
Axes of the slice: x: 2, y: 2, z: 4, core: 2. Of those that a mesh axis runs over, the one named last changes fastest.
Arguments:
- queries: bfloat16 [2560, 4096], P(('groups', 'ctx')), parts along dimension 0, may hold values from -200 to 200
- fresh_key_value: bfloat16 [2, 2560, 512], P(None, ('groups', 'ctx')), parts along dimension 1, may hold values from -6 to 6
- cache_key_value: bfloat16 [2, 4096, 512], P(None, ('groups', 'ctx')), parts along dimension 1, may hold values from -6 to 6
- residual: bfloat16 [2560, 2048], P(('groups', 'ctx')), parts along dimension 0, may hold values from -6 to 6
- norm_gain: float32 [2048], replicated, may hold values from 0.5 to 2
- out_proj: bfloat16 [4096, 2048], P('ctx'), may hold values from -0.09375 to 0.09375
- w_gate_up: bfloat16 [32, 2048, 1536], P('ctx'), may hold values from -0.125 to 0.125
- w_down: bfloat16 [32, 768, 2048], P('ctx'), may hold values from -0.21875 to 0.21875
- route_ids: int32 [2560, 8], P(('groups', 'ctx')), parts along dimension 0, may hold values from 0 to 31, all different within a row; in each aligned block of 80 rows (0 to 79, 80 to 159, ...) at most 30 rows name the same one
- route_weights: float32 [2560, 8], P(('groups', 'ctx')), parts along dimension 0, may hold values from 0.05 to 1
- placement: int32 [32], replicated, may hold values from 0 to 31, each once
Outputs:
- hidden: bfloat16 [2560, 2048], P(('groups', 'ctx')), parts along dimension 0
- expert_out: bfloat16 [2560, 2048], P(('groups', 'ctx')), parts along dimension 0
The draws below stay inside these ranges and needn't reach their ends.
There are 2 independent parts, one for each index of `groups`. The reference program is written for one: setup_inputs(seed, part) draws one part's arguments, and reference() takes and returns one part's arrays. A program takes and returns all parts, laid end to end along the dimension named above; an argument that names none is the same for every part. Nothing has to cross between parts.
Inputs may be any that keep to these rules, and one draw needn't show every extreme that they name: `route_ids`: among the rows of one index of ctx, no expert is named by more than 30 rows, a bound that some block reaches. `placement`: every slot once; slot s is the first index of w_gate_up and w_down.
All inputs are finite; a program needn't handle non-finite values.
Results may differ from the reference program's by a relative error of at most 0.017.
Values may be sent and summed in bfloat16 or wider, within the bound.
No kernel may reach another device: no remote copies, remote signals or barrier semaphores. Data moves between devices by JAX's collectives and lax.ppermute only.
A program may use at most 128 MiB of HBM per device.

```python
import math
import jax
import jax.numpy as jnp
import numpy as np
from jax import lax

D = 2048
QUERY_HEADS = 32
KEY_VALUE_HEADS = 4
HEAD_SIZE = 128
FF = 768
TOPK = 8
ROWS_DEV = 80
EXPERTS = 32
WINDOW_ROWS = 1280
CACHED_KEYS = 2048
MOST = 30
N_CTX = 16


def attention_pair(key):
    query_key = jax.random.fold_in(key, 101)
    stored_key = jax.random.fold_in(key, 102)
    random_value_key = jax.random.fold_in(key, 103)
    queries = 2.5 * jax.random.truncated_normal(query_key, -6.0, 6.0, (WINDOW_ROWS, QUERY_HEADS * HEAD_SIZE), jnp.float32)
    stored_keys = jax.random.truncated_normal(stored_key, -6.0, 6.0, (CACHED_KEYS, KEY_VALUE_HEADS * HEAD_SIZE), jnp.float32)
    stored_values = jax.random.truncated_normal(random_value_key, -6.0, 6.0, (CACHED_KEYS, KEY_VALUE_HEADS * HEAD_SIZE), jnp.float32)
    return (queries, stored_keys, stored_values)


def draw_queries(key, part):
    queries, stored_keys, stored_values = attention_pair(key)
    return queries.astype(jnp.bfloat16)


def draw_cache_key_value(key, part):
    queries, stored_keys, stored_values = attention_pair(key)
    return jnp.stack([stored_keys, stored_values], axis=0).astype(jnp.bfloat16)


def level_of(rng, dims, cuts, low, high):
    level = 1.0
    for dim, blocks in cuts:
        steps = jax.random.uniform(jax.random.fold_in(jax.random.fold_in(rng, 6), dim), (blocks,), jnp.float32, low / len(cuts), high / len(cuts))
        level = level * jnp.repeat(jnp.exp(steps), dims[dim] // blocks).reshape((-1,) + (1,) * (len(dims) - 1 - dim))
    return level


def routed_block(own_key, own, number, rows, number_of, top, reach, slope):
    ranking = jax.random.permutation(own_key, number_of)
    heavy_load, common = shares(number_of, rows * top, reach, slope, True), shares(number_of, rows * top, reach, slope, False)
    places = jnp.arange(number_of)

    def named(sizes, turn):
        used = int((sizes > 0).sum())
        fixed = max(1, used // 4)
        shifted = fixed + (places - fixed + turn * (used - fixed)) % max(1, number_of - fixed)
        return jnp.zeros((number_of,), jnp.int32).at[ranking[jnp.where(places < fixed, places, shifted)]].set(jnp.asarray(sizes, jnp.int32))

    sizes = jnp.where(number % 4 == 0, named(heavy_load, number // 4), named(common, number - number // 4 - 1))
    mixed = jax.random.permutation(jax.random.fold_in(own, 3), number_of)
    giver, taker = mixed[0:number_of // 2 * 2:2], mixed[1:number_of // 2 * 2:2]
    margin = jnp.minimum(sizes[giver] - 1, reach - sizes[taker]) // 2
    margin = jnp.where((giver == ranking[0]) | (taker == ranking[0]) | (sizes[taker] == 0), 0, jnp.maximum(margin, 0))
    shifted = jax.random.randint(jax.random.fold_in(own, 4), (number_of // 2,), 0, 1 << 20) % (margin + 1)
    sizes = sizes.at[giver].add(-shifted).at[taker].add(shifted)
    labels = jnp.searchsorted(jnp.cumsum(sizes), jnp.arange(rows * top), side="right").astype(jnp.int32)
    listing = labels.reshape(top, rows).T
    listing = listing[jax.random.permutation(jax.random.fold_in(own, 1), rows)]
    turn = jax.random.randint(jax.random.fold_in(own, 2), (rows, 1), 0, top)
    return jnp.take_along_axis(listing, (jnp.arange(top)[None, :] + turn) % top, axis=1)


def shares(number_of, total, bound, lean, full):
    weights = [(1 << 20) // math.isqrt(rank ** lean) + 1 for rank in range(1, number_of + 1)]
    largest = bound if full else min(bound, max(-(-total // number_of), total * weights[0] // sum(weights)))
    least = 1 if total - largest >= number_of - 1 else 0
    holding, surplus = [largest] + [least] * (number_of - 1), total - largest - least * (number_of - 1)
    while surplus > 0:
        candidates = [i for i in range(1, number_of) if holding[i] < largest] or [i for i in range(1, number_of) if holding[i] < bound]
        whole, remaining = sum([weights[i] for i in candidates]), surplus
        for i in candidates:
            addition = min(bound - holding[i], max(1, remaining * weights[i] // whole), surplus)
            holding[i] = holding[i] + addition
            surplus = surplus - addition
    return np.array(holding)


def centred(own_key, extent, spread, most, cuts=(), kind=jnp.bfloat16):
    values = jax.random.normal(own_key, extent, jnp.float32) * spread
    if len(cuts) > 0:
        values = level_of(own_key, extent, cuts, -0.22, 0.18) * values
    return jnp.clip(values, min=-most, max=most).astype(kind)


def setup_inputs(seed: int = 0, part: int = 0) -> dict:
    key_list = jax.random.split(jax.random.key(seed), 12)
    part_keys = jax.random.split(jax.random.fold_in(key_list[11], part), 12)
    queries = draw_queries(jax.random.fold_in(jax.random.fold_in(key_list[11], part), 71), part)
    fresh_key_value = centred(part_keys[1], (2, WINDOW_ROWS, KEY_VALUE_HEADS * HEAD_SIZE), 1.0, 6.0, ((1, 16),))
    cache_key_value = draw_cache_key_value(jax.random.fold_in(jax.random.fold_in(key_list[11], part), 71), part)
    residual = centred(part_keys[3], (WINDOW_ROWS, D), 1.0, 6.0, ((0, 16),))
    norm_gain = jnp.clip(jnp.exp(jax.random.uniform(key_list[4], (D,), jnp.float32, math.log(0.5), math.log(2.0))), 0.5, 2.0)
    out_proj = centred(key_list[5], (QUERY_HEADS * HEAD_SIZE, D), (QUERY_HEADS * HEAD_SIZE) ** -0.5, 0.09375, ((0, 16),))
    w_gate_up = centred(key_list[6], (EXPERTS, D, 2 * FF), D ** -0.5, 0.125, ((0, 16),))
    w_down = centred(key_list[7], (EXPERTS, FF, D), FF ** -0.5, 0.21875, ((0, 16),))
    route_ids_keys = jax.random.split(jax.random.fold_in(part_keys[8], 1), WINDOW_ROWS // ROWS_DEV)
    route_ids_turns = jax.random.permutation(jax.random.fold_in(part_keys[8], 3), WINDOW_ROWS // ROWS_DEV)
    route_ids = jax.vmap(lambda own, number: routed_block(jax.random.fold_in(part_keys[8], 2), own, number, ROWS_DEV, EXPERTS, TOPK, MOST, 2))(route_ids_keys, route_ids_turns).reshape((WINDOW_ROWS, TOPK))
    route_weights = jnp.clip(jnp.exp(math.log(1.0) - 2.9957323 * jax.random.uniform(part_keys[9], (WINDOW_ROWS, TOPK), jnp.float32) ** level_of(part_keys[9], (WINDOW_ROWS, TOPK), ((0, 16),), -0.2, 0.2)), 0.05, 1.0)
    placement = jax.random.permutation(key_list[10], EXPERTS).astype(jnp.int32)
    return dict(queries=queries, fresh_key_value=fresh_key_value, cache_key_value=cache_key_value, residual=residual, norm_gain=norm_gain, out_proj=out_proj, w_gate_up=w_gate_up, w_down=w_down, route_ids=route_ids, route_weights=route_weights, placement=placement)


def reference(queries, fresh_key_value, cache_key_value, residual, norm_gain, out_proj, w_gate_up, w_down, route_ids, route_weights, placement):
    count_of_rows = queries.shape[0]
    query_group_width = QUERY_HEADS // KEY_VALUE_HEADS
    scale_for_scores = HEAD_SIZE ** (-0.5)
    stored_keys = cache_key_value[0].astype(jnp.float32).reshape(-1, KEY_VALUE_HEADS, HEAD_SIZE)
    stored_values = cache_key_value[1].astype(jnp.float32).reshape(-1, KEY_VALUE_HEADS, HEAD_SIZE)
    block_of_rows = math.gcd(count_of_rows, 128)

    def attend(pieces):
        block_of_queries, self_key, self_value = pieces
        widened_query = block_of_queries.astype(jnp.float32).reshape(block_of_rows, KEY_VALUE_HEADS, query_group_width, HEAD_SIZE)
        scores = jnp.einsum('rkgd,jkd->rkgj', widened_query, stored_keys) * scale_for_scores
        self_score = jnp.einsum('ejaz,ejz->eja', widened_query, self_key.astype(jnp.float32).reshape(block_of_rows, KEY_VALUE_HEADS, HEAD_SIZE)) * scale_for_scores
        peak_value = jnp.maximum(lax.optimization_barrier(jnp.max(scores, axis=-1)), self_score)
        weights = jnp.exp(scores - peak_value[..., None])
        self_weight = jnp.exp(self_score - peak_value)
        totals = lax.optimization_barrier(jnp.sum(weights, axis=-1)) + self_weight
        weighted_total = jnp.einsum('rkgj,jkd->rkgd', weights.astype(jnp.bfloat16).astype(jnp.float32), stored_values)
        weighted_total = weighted_total + self_weight[..., None] * self_value.astype(jnp.float32).reshape(block_of_rows, KEY_VALUE_HEADS, 1, HEAD_SIZE)
        return (weighted_total / totals[..., None]).reshape(block_of_rows, QUERY_HEADS * HEAD_SIZE).astype(jnp.bfloat16)

    def blocked(array):
        return array.reshape(count_of_rows // block_of_rows, block_of_rows, array.shape[-1])
    attention = lax.map(attend, (blocked(queries), blocked(fresh_key_value[0]), blocked(fresh_key_value[1]))).reshape(count_of_rows, QUERY_HEADS * HEAD_SIZE)
    projected = jnp.dot(attention, out_proj, preferred_element_type=jnp.float32)
    hidden = (residual.astype(jnp.float32) + projected).astype(jnp.bfloat16)
    hidden_wide = hidden.astype(jnp.float32)
    normed = (hidden_wide * lax.rsqrt(lax.optimization_barrier(jnp.mean(hidden_wide * hidden_wide, axis=-1, keepdims=True)) + 1e-06) * norm_gain).astype(jnp.bfloat16)
    expert_count = placement.shape[0]
    slot_ids = placement[route_ids].reshape(-1).astype(jnp.int32)
    assigned = slot_ids.shape[0]
    sorted_idx = jnp.argsort(slot_ids, stable=True).astype(jnp.int32)
    expert_range = jnp.arange(expert_count, dtype=jnp.int32)
    counts = lax.optimization_barrier(jnp.sum((slot_ids[:, None] == expert_range[None, :]).astype(jnp.int32), axis=0)).astype(jnp.int32)
    starts = (jnp.cumsum(counts) - counts).astype(jnp.int32)
    capacity = N_CTX * MOST
    offsets = jnp.arange(capacity, dtype=jnp.int32)
    picked = jnp.minimum(starts[:, None] + offsets[None, :], assigned - 1).astype(jnp.int32)
    filled = offsets[None, :] < counts[:, None]
    source_rows = (sorted_idx[picked] // TOPK).astype(jnp.int32)

    def expert_run(pieces):
        slot_index, row_index, keep_rows = pieces
        inputs = jnp.where(keep_rows[:, None], normed[row_index], jnp.zeros((), jnp.bfloat16))
        both = jnp.dot(inputs, w_gate_up[slot_index], preferred_element_type=jnp.float32)
        active = (jax.nn.silu(both[:, :FF]) * both[:, FF:]).astype(jnp.bfloat16)
        return jnp.dot(active, w_down[slot_index], preferred_element_type=jnp.float32).astype(jnp.bfloat16)
    results = lax.map(expert_run, (expert_range, source_rows, filled))
    ranks = jnp.zeros((assigned,), jnp.int32).at[sorted_idx].set(jnp.arange(assigned, dtype=jnp.int32) - starts[slot_ids[sorted_idx]])
    routed = results[slot_ids, ranks].reshape(count_of_rows, TOPK, D).astype(jnp.float32)
    gate_share = route_weights / lax.optimization_barrier(jnp.sum(route_weights, axis=-1, keepdims=True))
    expert_out = lax.optimization_barrier(jnp.sum(gate_share[..., None] * routed, axis=1)).astype(jnp.bfloat16)
    return (hidden, expert_out)
```

```python
import functools
import math

import jax
import jax.numpy as jnp
from jax import lax
from jax.experimental import pallas as pl
from jax.experimental.pallas import tpu as pltpu
from jax.sharding import PartitionSpec as P

KEY_VALUE_HEADS = 4
HEAD_SIZE = 128
LANES = 128
EPSILON = 1e-06
MIB = 1 << 20


def rotation(inner, by):
    n = KEY_VALUE_HEADS
    return [(o * inner + t, ((o + by) % n) * inner + t) for o in range(n) for t in range(inner)]


def swap(inner, bit):
    return [
        (o * inner + t, o * inner + (t ^ bit)) for o in range(KEY_VALUE_HEADS) for t in range(inner)
    ]


def gather_inner(array, inner):
    pieces = {0: array}
    bit = inner // 2
    while bit:
        for j in list(pieces):
            pieces[j | bit] = lax.ppermute(pieces[j], "ctx", swap(inner, bit))
        bit //= 2
    return [pieces[j] for j in range(inner)]


def pack_kernel(inner, spot, queries, fresh, cache, ids, weights, placement, *outs):
    outer, place = spot[0], spot[1]
    rows = queries.shape[0]
    keys = cache.shape[1]
    group = queries.shape[1] // (KEY_VALUE_HEADS * HEAD_SIZE)
    per_device = group // inner
    experts = placement.shape[1]
    part = experts // KEY_VALUE_HEADS
    share = weights[...] / jnp.sum(weights[...], axis=-1, keepdims=True)
    expert = lax.broadcasted_iota(jnp.int32, (rows, experts), 1)
    gates = jnp.zeros((rows, experts), jnp.float32)
    for k in range(ids.shape[1]):
        gates += jnp.where(ids[:, k : k + 1] == expert, share[:, k : k + 1], 0.0)
    high = gates.astype(jnp.bfloat16)
    low = (gates - high.astype(jnp.float32)).astype(jnp.bfloat16)
    lane = lax.broadcasted_iota(jnp.int32, (LANES, experts), 0)
    slot = jnp.broadcast_to(placement[...], (LANES, experts))
    contract = (((1,), (1,)), ((), ()))
    for k in range(KEY_VALUE_HEADS):
        to = lax.rem(outer + k, KEY_VALUE_HEADS)
        kvg, qf = outs[2 * k], outs[2 * k + 1]
        column = pl.ds(pl.multiple_of(to * HEAD_SIZE, HEAD_SIZE), HEAD_SIZE)
        kvg[0:keys, :] = cache[0, :, column]
        kvg[keys : 2 * keys, :] = cache[1, :, column]
        first = to * part
        half = LANES // 2
        pick_high = jnp.where((slot == first + lane) & (lane < part), 1.0, 0.0)
        pick_low = jnp.where((slot == first + lane - half) & (lane >= half) & (lane < half + part), 1.0, 0.0)
        block = lax.dot_general(
            high, pick_high.astype(jnp.bfloat16), contract, preferred_element_type=jnp.float32
        ) + lax.dot_general(
            low, pick_low.astype(jnp.bfloat16), contract, preferred_element_type=jnp.float32
        )
        kvg[2 * keys :, :] = block.astype(jnp.bfloat16)
        for h in range(group):
            head = to * group + (place ^ (h // per_device)) * per_device + h % per_device
            qf[h * rows : (h + 1) * rows, :] = queries[
                :, pl.ds(pl.multiple_of(head * HEAD_SIZE, HEAD_SIZE), HEAD_SIZE)
            ]
        qf[group * rows : (group + 1) * rows, :] = fresh[0, :, column]
        qf[(group + 1) * rows :, :] = fresh[1, :, column]


def merge_kernel(keys, *refs):
    out = refs[-1]
    n = len(refs) - 1
    rows = refs[0].shape[0] - 2 * keys
    start = n * rows
    for k in range(n):
        out[k * rows : (k + 1) * rows, :] = refs[k][2 * keys :, :]
        out[start + k * keys : start + (k + 1) * keys, :] = refs[k][:keys, :]
        out[start + (n + k) * keys : start + (n + k + 1) * keys, :] = refs[k][keys : 2 * keys, :]


def attention_kernel(inner, group, rows, block_keys, qf, *refs):
    caches, projections, out = refs[:inner], refs[inner : 2 * inner], refs[2 * inner]
    keys, values, attention = refs[2 * inner + 1 :]
    for j in range(inner):
        start = caches[j].shape[0] - 2 * block_keys
        keys[j * block_keys : (j + 1) * block_keys, :] = caches[j][start : start + block_keys, :]
        values[j * block_keys : (j + 1) * block_keys, :] = caches[j][start + block_keys :, :]
    factor = HEAD_SIZE ** (-0.5) * math.log2(math.e)
    own_key = qf[group * rows : (group + 1) * rows, :].astype(jnp.float32)
    own_value = qf[(group + 1) * rows :, :].astype(jnp.float32)
    step = max(1, group // 2)
    for h0 in range(0, group, step):
        query = qf[h0 * rows : (h0 + step) * rows, :]
        own = (
            jnp.sum(
                query.astype(jnp.float32) * jnp.concatenate([own_key] * step, axis=0),
                axis=-1,
                keepdims=True,
            )
            * factor
        )
        scores = (
            lax.dot_general(
                query, keys[...], (((1,), (1,)), ((), ())), preferred_element_type=jnp.float32
            )
            * factor
        )
        peak = jnp.maximum(own, jnp.max(scores, axis=-1, keepdims=True))
        weights = jnp.exp2(scores - peak)
        own = jnp.exp2(own - peak)
        totals = jnp.sum(weights, axis=-1, keepdims=True) + own
        weighted = jnp.dot(
            weights.astype(jnp.bfloat16), values[...], preferred_element_type=jnp.float32
        )
        weighted = weighted + own * jnp.concatenate([own_value] * step, axis=0)
        result = (weighted / totals).astype(jnp.bfloat16)
        for h in range(step):
            attention[:, (h0 + h) * HEAD_SIZE : (h0 + h + 1) * HEAD_SIZE] = result[
                h * rows : (h + 1) * rows, :
            ]
    depth = projections[0].shape[0]
    total = jnp.zeros(out.shape, jnp.float32)
    for j in range(inner):
        total += jnp.dot(
            attention[:, j * depth : (j + 1) * depth],
            projections[j][...],
            preferred_element_type=jnp.float32,
        )
    out[...] = total.astype(out.dtype)


def norm_kernel(residual, gain, own, *refs):
    arrived, (hidden, normed) = refs[:-2], refs[-2:]
    total = own[...]
    for ref in arrived:
        total = total + ref[...].astype(jnp.float32)
    rounded = (residual[...].astype(jnp.float32) + total).astype(jnp.bfloat16)
    hidden[...] = rounded
    wide = rounded.astype(jnp.float32)
    scale = lax.rsqrt(jnp.mean(wide * wide, axis=-1, keepdims=True) + EPSILON)
    normed[...] = (wide * scale * gain[...]).astype(jnp.bfloat16)


def expert_kernel(inner, local, spot, *refs):
    pieces, gates = refs[:inner], refs[inner : 2 * inner]
    gate, up, down, keep, send, total, stacked = refs[2 * inner :]
    expert, tile = pl.program_id(0), pl.program_id(1)
    rows = pieces[0].shape[0]
    order = halves(inner)

    @pl.when((expert == 0) & (tile == 0))
    def first():
        for at, j in enumerate(order):
            stacked[at * rows : (at + 1) * rows, :] = pieces[j][...]
        total[...] = jnp.zeros_like(total)

    lane = lax.broadcasted_iota(jnp.int32, (rows, LANES), 1)
    column = spot[1] * local + expert
    mine = (lane == column) | (lane == column + LANES // 2)
    share = jnp.concatenate(
        [
            jnp.sum(
                jnp.where(mine, gates[j][...].astype(jnp.float32), 0.0), axis=-1, keepdims=True
            )
            for j in order
        ],
        axis=0,
    )
    rows_in = stacked[...]
    left = jnp.dot(rows_in, gate[0], preferred_element_type=jnp.float32)
    right = jnp.dot(rows_in, up[0], preferred_element_type=jnp.float32)
    active = (left / (1.0 + jnp.exp(-left)) * right * share).astype(jnp.bfloat16)
    total[...] += jnp.dot(active, down[0], preferred_element_type=jnp.float32)

    @pl.when((expert == pl.num_programs(0) - 1) & (tile == pl.num_programs(1) - 1))
    def last():
        half = keep.shape[0]
        keep[...] = total[:half, :].astype(keep.dtype)
        send[...] = total[half:, :].astype(send.dtype)


def halves(inner):
    order, bit = [0], inner // 2
    while bit:
        order = order + [j | bit for j in order]
        bit //= 2
    return order


def whole(shape):
    return pl.BlockSpec(shape, lambda *_: (0,) * len(shape))


def vmem(count):
    return [pl.BlockSpec(memory_space=pltpu.VMEM)] * count


def local_program(
    n,
    queries,
    fresh,
    cache,
    residual,
    gain,
    out_proj,
    w_gate_up,
    w_down,
    route_ids,
    route_weights,
    placement,
):
    bf16, f32 = jnp.bfloat16, jnp.float32
    outers = KEY_VALUE_HEADS
    inner = n // outers
    rows, width = residual.shape
    keys = cache.shape[1]
    group = queries.shape[1] // (outers * HEAD_SIZE)
    local, _, both = w_gate_up.shape
    ff = both // 2
    me = lax.axis_index("ctx")
    spot = jnp.stack([me // inner, me % inner]).astype(jnp.int32)
    smem = pl.BlockSpec(memory_space=pltpu.SMEM)

    def params(limit):
        return pltpu.CompilerParams(vmem_limit_bytes=limit * MIB)

    kvg_rows, qf_rows = 2 * keys + rows, (group + 2) * rows
    packed = pl.pallas_call(
        functools.partial(pack_kernel, inner),
        out_shape=[
            jax.ShapeDtypeStruct((size, HEAD_SIZE), bf16)
            for _ in range(outers)
            for size in (kvg_rows, qf_rows)
        ],
        in_specs=[smem] + vmem(6),
        out_specs=vmem(2 * outers),
        compiler_params=params(16),
        name="pack",
    )(spot, queries, fresh, cache, route_ids, route_weights, placement.reshape(1, -1))
    projections = gather_inner(out_proj, inner)
    kvg = [packed[0]] + [
        lax.ppermute(packed[2 * k], "ctx", rotation(inner, k)) for k in range(1, outers)
    ]
    qf = [packed[1]] + [
        lax.ppermute(packed[2 * k + 1], "ctx", rotation(inner, k)) for k in range(1, outers)
    ]
    merged = pl.pallas_call(
        functools.partial(merge_kernel, keys),
        out_shape=jax.ShapeDtypeStruct((outers * kvg_rows, HEAD_SIZE), bf16),
        in_specs=vmem(outers),
        out_specs=pl.BlockSpec(memory_space=pltpu.VMEM),
        name="merge",
    )(*kvg)
    caches = gather_inner(merged, inner)

    def attend(k):
        return pl.pallas_call(
            functools.partial(attention_kernel, inner, group, rows, outers * keys),
            out_shape=jax.ShapeDtypeStruct((rows, width), f32 if k == 0 else bf16),
            in_specs=vmem(1 + 2 * inner),
            out_specs=pl.BlockSpec(memory_space=pltpu.VMEM),
            scratch_shapes=[
                pltpu.VMEM((n * keys, HEAD_SIZE), bf16),
                pltpu.VMEM((n * keys, HEAD_SIZE), bf16),
                pltpu.VMEM((rows, group * HEAD_SIZE), bf16),
            ],
            compiler_params=params(40),
            cost_estimate=pl.CostEstimate(
                flops=4 * group * rows * n * keys * HEAD_SIZE
                + 2 * rows * group * HEAD_SIZE * width,
                bytes_accessed=6 * MIB,
                transcendentals=group * rows * n * keys,
            ),
            name="attention",
        )(qf[k], *caches, *projections)

    home = [
        lax.ppermute(attend(k), "ctx", rotation(inner, -k)) if k else attend(k)
        for k in [*range(1, outers), 0]
    ]
    hidden, normed = pl.pallas_call(
        norm_kernel,
        out_shape=[jax.ShapeDtypeStruct((rows, width), bf16)] * 2,
        in_specs=vmem(2 + outers),
        out_specs=vmem(2),
        compiler_params=params(16),
        name="norm",
    )(residual, gain.reshape(1, -1), home[-1], *home[:-1])

    tile = 256 if ff % 256 == 0 else ff
    tiles = ff // tile
    half = rows * inner // 2

    def experts(k, pieces):
        return pl.pallas_call(
            functools.partial(expert_kernel, inner, local),
            grid=(local, tiles),
            out_shape=[jax.ShapeDtypeStruct((half, width), bf16)] * 2,
            in_specs=[smem]
            + [whole((rows, width))] * inner
            + [pl.BlockSpec((rows, LANES), lambda *_: (k, 0))] * inner
            + [
                pl.BlockSpec((1, width, tile), lambda e, f: (e, 0, f)),
                pl.BlockSpec((1, width, tile), lambda e, f: (e, 0, f + tiles)),
                pl.BlockSpec((1, tile, width), lambda e, f: (e, f, 0)),
            ],
            out_specs=[whole((half, width))] * 2,
            scratch_shapes=[
                pltpu.VMEM((rows * inner, width), f32),
                pltpu.VMEM((rows * inner, width), bf16),
            ],
            compiler_params=params(48),
            cost_estimate=pl.CostEstimate(
                flops=6 * rows * inner * width * ff * local,
                bytes_accessed=6 * width * ff * local,
                transcendentals=rows * inner * ff * local,
            ),
            name="experts",
        )(spot, *pieces, *caches, w_gate_up, w_gate_up, w_down)

    def reduce_inner(keep, send):
        bit = 1
        while True:
            arrived = lax.ppermute(send, "ctx", swap(inner, bit))
            total = keep.astype(f32) + arrived.astype(f32)
            bit *= 2
            if bit == inner:
                return total
            middle = total.shape[0] // 2
            keep, send = total[:middle], total[middle:].astype(bf16)

    result = None
    order = [0] + list(range(1, outers))
    sources = [normed] + [
        lax.ppermute(normed, "ctx", rotation(inner, k)) for k in range(1, outers)
    ]
    for k in order:
        keep, send = experts(k, gather_inner(sources[k], inner))
        total = reduce_inner(keep, send)
        if k:
            total = lax.ppermute(total.astype(bf16), "ctx", rotation(inner, -k)).astype(f32)
        result = total if result is None else result + total
    return hidden, result.astype(bf16)


def solution(mesh):
    rows = P(("groups", "ctx"), None)
    middle = P(None, ("groups", "ctx"), None)
    in_specs = (
        rows,
        middle,
        middle,
        rows,
        P(),
        P("ctx", None),
        P("ctx", None, None),
        P("ctx", None, None),
        rows,
        rows,
        P(),
    )
    return jax.shard_map(
        functools.partial(local_program, mesh.shape["ctx"]),
        mesh=mesh,
        in_specs=in_specs,
        out_specs=(rows, rows),
        check_vma=False,
    )
```

```python
import functools
import math

import jax
import jax.numpy as jnp
from jax import lax
from jax.experimental import pallas as pl
from jax.experimental.pallas import tpu as pltpu
from jax.sharding import PartitionSpec as P

OUTERS = 4
HEAD_SIZE = 128
LANES = 128
EPSILON = 1e-06
MIB = 1 << 20
BF16, F32 = jnp.bfloat16, jnp.float32
NT = (((1,), (1,)), ((), ()))
ANY = pl.BlockSpec(memory_space=pl.ANY)
VMEM = pl.BlockSpec(memory_space=pltpu.VMEM)
SMEM = pl.BlockSpec(memory_space=pltpu.SMEM)


def swap(array, n, offset):
    return lax.ppermute(array, "ctx", [(i, i ^ offset) for i in range(n)])


def gather_inner(array, n, *tokens):
    pieces = {0: array}
    bit = n // OUTERS // 2
    while bit:
        for j in list(pieces):
            ready = lax.optimization_barrier((pieces[j], *tokens))[0] if j and tokens else pieces[j]
            pieces[j | bit] = swap(ready, n, bit)
        bit //= 2
    return [pieces[j] for j in range(n // OUTERS)]


def halves(inner):
    order, bit = [0], inner // 2
    while bit:
        order = order + [j | bit for j in order]
        bit //= 2
    return order


def call(kernel, outs, operands, specs, name, tokens=(), limit=16, scratch=(), out_specs=None, grid=None, cost=True):
    count = len(operands)

    def body(*refs):
        kernel(*refs[:count], *refs[count + len(tokens) :])

    more = {} if grid is None else {"grid": grid}
    return pl.pallas_call(
        body,
        out_shape=outs,
        in_specs=list(specs) + [ANY] * len(tokens),
        out_specs=out_specs,
        scratch_shapes=list(scratch),
        compiler_params=pltpu.CompilerParams(vmem_limit_bytes=limit * MIB),
        cost_estimate=pl.CostEstimate(flops=1, bytes_accessed=1, transcendentals=0),
        name=name,
        **more,
    )(*operands, *tokens)


def whole(shape):
    return pl.BlockSpec(shape, lambda *_: (0,) * len(shape))


def start_all(pairs, sems):
    copies = [
        pltpu.make_async_copy(src, dst, sems.at[at]) for at, (src, dst) in enumerate(pairs)
    ]
    for copy in copies:
        copy.start()
    return copies


def wait_all(copies):
    for copy in copies:
        copy.wait()


def pack_kernel(inner, spot, *refs):
    sources, refs = refs[:6], refs[6:]
    outs, made = refs[:OUTERS], refs[OUTERS : 2 * OUTERS]
    queries, fresh, cache, ids, weights, placement, sems, last = refs[2 * OUTERS :]
    landed = (queries, fresh, cache, ids, weights, placement)
    copies = start_all(list(zip(sources, landed))[::-1], sems)[::-1]
    wait_all(copies[2:])
    outer, place = spot[0], spot[1]
    rows = queries.shape[0]
    keys = cache.shape[1]
    group = queries.shape[1] // (OUTERS * HEAD_SIZE)
    per_device = group // inner
    experts = placement.shape[1]
    part = experts // OUTERS
    share = weights[...] / jnp.sum(weights[...], axis=0, keepdims=True)
    expert = lax.broadcasted_iota(jnp.int32, (experts, rows), 0)
    gates = jnp.zeros((experts, rows), F32)
    for k in range(ids.shape[0]):
        gates += jnp.where(ids[k : k + 1, :] == expert, share[k : k + 1, :], 0.0)
    gates = gates.T
    high = gates.astype(BF16)
    low = (gates - high.astype(F32)).astype(BF16)
    lane = lax.broadcasted_iota(jnp.int32, (LANES, experts), 0)
    slot = jnp.broadcast_to(placement[...], (LANES, experts))
    half = LANES // 2
    sent = []
    wait_all(copies[:2])
    for k in [1, 2, 3, 0]:
        to = outer ^ k
        block = made[k]
        column = pl.ds(pl.multiple_of(to * HEAD_SIZE, HEAD_SIZE), HEAD_SIZE)
        block[0:keys, :] = cache[0, :, column]
        block[keys : 2 * keys, :] = cache[1, :, column]
        first = to * part
        pick_high = jnp.where((slot == first + lane) & (lane < part), 1.0, 0.0)
        pick_low = jnp.where(
            (slot == first + lane - half) & (lane >= half) & (lane < half + part), 1.0, 0.0
        )
        wanted = lax.dot_general(
            high, pick_high.astype(BF16), NT, preferred_element_type=F32
        ) + lax.dot_general(low, pick_low.astype(BF16), NT, preferred_element_type=F32)
        at = 2 * keys + rows
        block[2 * keys : at, :] = wanted.astype(BF16)
        for h in range(group):
            head = to * group + (place ^ (h // per_device)) * per_device + h % per_device
            block[at : at + rows, :] = queries[
                :, pl.ds(pl.multiple_of(head * HEAD_SIZE, HEAD_SIZE), HEAD_SIZE)
            ]
            at += rows
        block[at : at + rows, :] = fresh[0, :, column]
        block[at + rows :, :] = fresh[1, :, column]
        copy = pltpu.make_async_copy(block, outs[k], last.at[k])
        copy.start()
        sent.append(copy)
    wait_all(sent)


def merge_kernel(keys, rows, *refs):
    blocks, out, sems = refs[:-2], refs[-2], refs[-1]
    count = len(blocks)
    start = count * rows
    pairs = []
    for k in range(count):
        for at, size, to in (
            (2 * keys, rows, k * rows),
            (0, keys, start + k * keys),
            (keys, keys, start + (count + k) * keys),
        ):
            pairs.append((blocks[k].at[pl.ds(at, size)], out.at[pl.ds(to, size)]))
    wait_all(start_all(pairs, sems))


def attention_kernel(inner, group, rows, packed, *refs):
    caches, projections = refs[: 2 * inner], refs[2 * inner : 3 * inner]
    out, keys, values, attention = refs[3 * inner :]
    block = keys.shape[0] // (2 * inner)
    start = caches[0].shape[0] - 2 * block
    for j in range(2 * inner):
        keys[j * block : (j + 1) * block, :] = caches[j][start : start + block, :]
        values[j * block : (j + 1) * block, :] = caches[j][start + block :, :]
    factor = HEAD_SIZE ** (-0.5) * math.log2(math.e)
    qf = packed.at[pl.ds(packed.shape[0] - (group + 2) * rows, (group + 2) * rows)]
    own_key = qf[group * rows : (group + 1) * rows, :].astype(F32)
    own_value = qf[(group + 1) * rows :, :].astype(F32)
    step = max(1, group // 2)
    for h0 in range(0, group, step):
        query = qf[h0 * rows : (h0 + step) * rows, :]
        own = jnp.sum(
            query.astype(F32) * jnp.concatenate([own_key] * step, axis=0), axis=-1, keepdims=True
        )
        scores = lax.dot_general(query, keys[...], NT, preferred_element_type=F32)
        peak = jnp.maximum(own, jnp.max(scores, axis=-1, keepdims=True)) * factor
        weights = jnp.exp2(scores * factor - peak)
        own = jnp.exp2(own * factor - peak)
        totals = jnp.sum(weights, axis=-1, keepdims=True) + own
        weighted = jnp.dot(weights.astype(BF16), values[...], preferred_element_type=F32)
        weighted = weighted + own * jnp.concatenate([own_value] * step, axis=0)
        block_out = (weighted / totals).astype(BF16)
        for h in range(step):
            attention[:, (h0 + h) * HEAD_SIZE : (h0 + h + 1) * HEAD_SIZE] = block_out[
                h * rows : (h + 1) * rows, :
            ]
    depth = projections[0].shape[0]
    wide = math.gcd(out.shape[1], 512)
    for c in range(0, out.shape[1], wide):
        total = jnp.dot(
            attention[:, :depth], projections[0][:, c : c + wide], preferred_element_type=F32
        )
        for j in range(1, inner):
            total += jnp.dot(
                attention[:, j * depth : (j + 1) * depth],
                projections[j][:, c : c + wide],
                preferred_element_type=F32,
            )
        out[:, c : c + wide] = total.astype(out.dtype)


def select_kernel(inner, local, capacity, spot, *refs):
    gates, (sel, selt, share) = refs[: 2 * inner], refs[2 * inner :]
    early = pl.program_id(0) < OUTERS // 2
    table = jnp.concatenate(
        [jnp.where(early, gates[j][...], gates[inner + j][...]) for j in halves(inner)], axis=0
    )
    rows = table.shape[0]
    first = spot[1] * local
    lane = lax.broadcasted_iota(jnp.int32, (LANES, LANES), 1)
    sub = lax.broadcasted_iota(jnp.int32, (LANES, LANES), 0)
    pick = jnp.where((lane == first + sub) & (sub < local), 1.0, 0.0).astype(BF16)
    across = lax.dot_general(pick[:16], table, NT, preferred_element_type=F32)
    down = lax.dot_general(table, pick, NT, preferred_element_type=F32)
    r = lax.broadcasted_iota(jnp.int32, (rows, rows), 0)
    c = lax.broadcasted_iota(jnp.int32, (rows, rows), 1)
    upper = jnp.where(r <= c, 1.0, 0.0).astype(BF16)
    lower = jnp.where(c <= r, 1.0, 0.0).astype(BF16)
    across_rank = jnp.dot(
        jnp.where(across > 0, 1.0, 0.0).astype(BF16), upper, preferred_element_type=F32
    )
    across_rank = jnp.where(across > 0, across_rank, 0.0)
    down_rank = jnp.dot(
        lower, jnp.where(down > 0, 1.0, 0.0).astype(BF16), preferred_element_type=F32
    )
    down_rank = jnp.where(down > 0, down_rank, 0.0)
    place = lax.broadcasted_iota(jnp.int32, (capacity, rows), 0).astype(F32) + 1.0
    place_t = lax.broadcasted_iota(jnp.int32, (rows, capacity), 1).astype(F32) + 1.0
    spread = lax.broadcasted_iota(jnp.int32, (capacity, LANES), 1)
    for e in range(local):
        chosen = jnp.where(across_rank[e : e + 1, :] == place, 1.0, 0.0).astype(BF16)
        sel[0, e * capacity : (e + 1) * capacity, :] = chosen
        selt[0, :, e * capacity : (e + 1) * capacity] = jnp.where(
            down_rank[:, e : e + 1] == place_t, 1.0, 0.0
        ).astype(BF16)
        mine = (spread == first + e) | (spread == first + e + LANES // 2)
        found = jnp.dot(chosen, table, preferred_element_type=F32)
        value = jnp.sum(jnp.where(mine, found, 0.0), axis=-1, keepdims=True)
        share[0, e * capacity : (e + 1) * capacity, :] = jnp.broadcast_to(value, (capacity, LANES))


def norm_kernel(residual, gain, own, *refs):
    arrived, (hidden, normed) = refs[:-2], refs[-2:]
    total = own[...]
    for ref in arrived:
        total = total + ref[...].astype(F32)
    rounded = (residual[...].astype(F32) + total).astype(BF16)
    hidden[...] = rounded
    wide = rounded.astype(F32)
    scale = lax.rsqrt(jnp.mean(wide * wide, axis=-1, keepdims=True) + EPSILON)
    normed[...] = (wide * scale * gain[...]).astype(BF16)


def expert_kernel(inner, chunk, *refs):
    pieces = refs[:inner]
    sel, selt, share, gate_up, down = refs[inner : inner + 5]
    sel, selt, share = sel.at[chunk], selt.at[chunk], share.at[chunk]
    outs = refs[inner + 5 : 2 * inner + 5]
    stacked, packed, active, made = refs[2 * inner + 5 :]
    local, width, both = gate_up.shape
    ff = both // 2
    rows = pieces[0].shape[0]
    capacity = sel.shape[0] // local
    for at, j in enumerate(halves(inner)):
        stacked[at * rows : (at + 1) * rows, :] = pieces[j][...]
    wide = math.gcd(width, 512)
    tile = math.gcd(ff, 256)
    for c in range(0, width, wide):
        packed[:, c : c + wide] = jnp.dot(
            sel[...], stacked[:, c : c + wide], preferred_element_type=F32
        ).astype(BF16)
    for e in range(local):
        at = slice(e * capacity, (e + 1) * capacity)
        for f in range(0, ff, tile):
            left = jnp.dot(packed[at, :], gate_up[e, :, f : f + tile], preferred_element_type=F32)
            right = jnp.dot(
                packed[at, :], gate_up[e, :, ff + f : ff + f + tile], preferred_element_type=F32
            )
            active[at, f : f + tile] = (left / (1.0 + jnp.exp(-left)) * right).astype(BF16)
        for c in range(0, width, wide):
            produced = jnp.dot(active[at, :], down[e, :, c : c + wide], preferred_element_type=F32)
            made[at, c : c + wide] = (produced * share[at, 0:1]).astype(BF16)
    for c in range(0, width, wide):
        total = jnp.dot(selt[...], made[:, c : c + wide], preferred_element_type=F32).astype(BF16)
        for at, out in enumerate(outs):
            out[:, c : c + wide] = total[at * rows : (at + 1) * rows, :]


def add_kernel(*refs):
    total = refs[0][...].astype(F32)
    for ref in refs[1:-1]:
        total = total + ref[...].astype(F32)
    refs[-1][...] = total.astype(refs[-1].dtype)


def local_program(
    n,
    queries,
    fresh,
    cache,
    residual,
    gain,
    out_proj,
    w_gate_up,
    w_down,
    route_ids,
    route_weights,
    placement,
):
    inner = n // OUTERS
    rows, width = residual.shape
    keys = cache.shape[1]
    group = queries.shape[1] // (OUTERS * HEAD_SIZE)
    local, _, both = w_gate_up.shape
    ff = both // 2
    experts_all = placement.shape[0]
    top = route_ids.shape[1]
    most = max(2, 3 * rows * top // (2 * experts_all))
    capacity = -(-most * inner // 16) * 16
    chunk_rows = rows * inner
    me = lax.axis_index("ctx")
    spot = jnp.stack([me // inner, me % inner]).astype(jnp.int32)
    dma = pltpu.SemaphoreType.DMA

    packed_rows = 2 * keys + rows + (group + 2) * rows
    ids_t, weights_t, slots = route_ids.T, route_weights.T, placement.reshape(1, -1)
    operands = (queries, fresh, cache, ids_t, weights_t, slots)
    packed = call(
        functools.partial(pack_kernel, inner),
        [jax.ShapeDtypeStruct((packed_rows, HEAD_SIZE), BF16)] * OUTERS,
        (spot, *operands),
        [SMEM] + [ANY] * 6,
        "pack",
        limit=60,
        out_specs=[ANY] * OUTERS,
        scratch=[
            *[pltpu.VMEM((packed_rows, HEAD_SIZE), BF16)] * OUTERS,
            *[pltpu.VMEM(a.shape, a.dtype) for a in operands],
            dma((6,)),
            dma((OUTERS,)),
        ],
    )
    blocks = [packed[0]] + [swap(packed[k], n, k * inner) for k in range(1, OUTERS)]
    half_outers = OUTERS // 2
    caches, tokens = [], ()
    for at in (0, half_outers):
        merged = call(
            functools.partial(merge_kernel, keys, rows),
            jax.ShapeDtypeStruct((half_outers * (2 * keys + rows), HEAD_SIZE), BF16),
            blocks[at : at + half_outers],
            [ANY] * half_outers,
            "merge",
            tokens,
            out_specs=ANY,
            scratch=[dma((3 * half_outers,))],
        )
        caches += gather_inner(merged, n)
        tokens = (caches[inner // 2],)
    projections = gather_inner(out_proj, n, merged)

    def add(terms, tokens=()):
        return call(
            add_kernel,
            jax.ShapeDtypeStruct((rows, width), BF16),
            terms,
            [VMEM] * len(terms),
            "add",
            tokens,
            out_specs=VMEM,
        )

    def attend(k, tokens, kind):
        return call(
            functools.partial(attention_kernel, inner, group, rows),
            jax.ShapeDtypeStruct((rows, width), kind),
            (blocks[k], *caches, *projections),
            [VMEM] * (1 + 3 * inner),
            "attention",
            tokens,
            limit=18,
            out_specs=VMEM,
            scratch=[
                pltpu.VMEM((n * keys, HEAD_SIZE), BF16),
                pltpu.VMEM((n * keys, HEAD_SIZE), BF16),
                pltpu.VMEM((rows, group * HEAD_SIZE), BF16),
            ],
        )

    selected = [
        (local * capacity, chunk_rows),
        (chunk_rows, local * capacity),
        (local * capacity, LANES),
    ]
    kinds = [BF16, BF16, F32]
    last_half = half_outers - 1
    far = attend(3, (), BF16)
    across = attend(2, (far,), F32)
    near = attend(1, (across,), BF16)
    sent = add([across, swap(far, n, inner)], (near,))
    own = attend(0, (sent,), F32)
    home = [swap(near, n, inner), swap(sent, n, 2 * inner)]
    selection = call(
        functools.partial(select_kernel, inner, local, capacity),
        [jax.ShapeDtypeStruct((OUTERS, *s), d) for s, d in zip(selected, kinds)],
        (spot, *caches),
        [SMEM]
        + [pl.BlockSpec((rows, LANES), lambda k: (jnp.minimum(k, last_half), 0))] * inner
        + [pl.BlockSpec((rows, LANES), lambda k: (jnp.maximum(k - half_outers, 0), 0))] * inner,
        "select",
        (own,),
        out_specs=[pl.BlockSpec((1, *s), lambda k: (k, 0, 0)) for s in selected],
        grid=(OUTERS,),
    )
    block = whole((rows, width))
    hidden, normed = call(
        norm_kernel,
        [jax.ShapeDtypeStruct((rows, width), BF16)] * 2,
        (residual, gain.reshape(1, -1), own, *home),
        [block, whole((1, width)), block, block, block],
        "norm",
        (selection[0],),
        out_specs=[block, block],
        grid=(1,),
    )

    def experts(k, pieces, tokens):
        return call(
            functools.partial(expert_kernel, inner, k),
            [jax.ShapeDtypeStruct((rows, width), BF16)] * inner,
            (*pieces, *selection, w_gate_up, w_down),
            [VMEM] * (inner + 5),
            "experts",
            tokens,
            limit=14,
            out_specs=[VMEM] * inner,
            scratch=[
                pltpu.VMEM((chunk_rows, width), BF16),
                pltpu.VMEM((local * capacity, width), BF16),
                pltpu.VMEM((local * capacity, ff), BF16),
                pltpu.VMEM((local * capacity, width), BF16),
            ],
        )

    bits = [1 << b for b in range(inner.bit_length() - 1)]
    first, second = swap(normed, n, inner), swap(normed, n, 2 * inner)
    around = gather_inner(normed, n)
    third = swap(second, n, inner)
    slots = [None] * OUTERS

    def fold(k):
        middle = len(slots[k]) // 2
        arrived = [swap(a, n, bits[0]) for a in slots[k][:middle - 1:-1]][::-1]
        slots[k] = [[a, b] for a, b in zip(slots[k][:middle], arrived)]

    def finish(k, tokens):
        terms = slots[k]
        for bit in bits[1:]:
            middle = len(terms) // 2
            sent = [add(t, tokens) for t in terms[middle:]]
            terms = [t + [swap(a, n, bit)] for t, a in zip(terms[:middle], sent)]
        return terms[0], sent[0]

    slots[0] = experts(0, around, ())
    fold(0)
    done = slots[0][0][0]
    slots[1] = experts(1, gather_inner(first, n, done), (done, second))
    fold(1)
    done = slots[1][0][0]
    slots[3] = experts(3, gather_inner(third, n, done), (done,))
    fold(3)
    done = slots[3][0][0]
    terms, sent = finish(3, (done,))
    slots[2] = experts(2, gather_inner(second, n, done), (sent,))
    fold(2)
    far = swap(add(terms, (slots[2][0][0],)), n, inner)
    terms, sent = finish(2, (slots[2][0][0],))
    total = add(terms + [far], (sent,))
    across = swap(total, n, 2 * inner)
    terms, sent = finish(1, (total,))
    total = add(terms, (sent,))
    near = swap(total, n, inner)
    terms, sent = finish(0, (total,))
    return hidden, add(terms + [near, across])


def solution(mesh):
    rows = P(("groups", "ctx"), None)
    middle = P(None, ("groups", "ctx"), None)
    in_specs = (
        rows,
        middle,
        middle,
        rows,
        P(),
        P("ctx", None),
        P("ctx", None, None),
        P("ctx", None, None),
        rows,
        rows,
        P(),
    )
    return jax.shard_map(
        functools.partial(local_program, mesh.shape["ctx"]),
        mesh=mesh,
        in_specs=in_specs,
        out_specs=(rows, rows),
        check_vma=False,
    )
```

```python
import functools
import math

import jax
import jax.numpy as jnp
from jax import lax
from jax.experimental import pallas as pl
from jax.experimental.pallas import tpu as pltpu
from jax.sharding import PartitionSpec as P

OUTERS = 4
HEAD_SIZE = 128
LANES = 128
EPSILON = 1e-06
MIB = 1 << 20
BF16, F32 = jnp.bfloat16, jnp.float32
NT = (((1,), (1,)), ((), ()))
ANY = pl.BlockSpec(memory_space=pl.ANY)
VMEM = pl.BlockSpec(memory_space=pltpu.VMEM)


def swap(array, n, offset):
    return lax.ppermute(array, "ctx", [(i, i ^ offset) for i in range(n)])


def after(array, *tokens):
    return lax.optimization_barrier((array, *tokens))[0]


def gather_inner(array, n, *tokens, far=None):
    pieces = {0: array}
    bit = n // OUTERS // 2
    if far is not None:
        pieces[bit] = far
    while bit:
        for j in list(pieces):
            if j | bit not in pieces:
                ready = after(pieces[j], *tokens) if j and tokens else pieces[j]
                pieces[j | bit] = swap(ready, n, bit)
        bit //= 2
    return [pieces[j] for j in range(n // OUTERS)]


def halves(inner):
    order, bit = [0], inner // 2
    while bit:
        order = order + [j | bit for j in order]
        bit //= 2
    return order


def call(kernel, outs, operands, specs, name, tokens=(), limit=16, scratch=(), out_specs=None, grid=None, cost=True):
    count = len(operands)

    def body(*refs):
        kernel(*refs[:count], *refs[count + len(tokens) :])

    more = {} if grid is None else {"grid": grid}
    return pl.pallas_call(
        body,
        out_shape=outs,
        in_specs=list(specs) + [ANY] * len(tokens),
        out_specs=out_specs,
        scratch_shapes=list(scratch),
        compiler_params=pltpu.CompilerParams(vmem_limit_bytes=limit * MIB),
        cost_estimate=pl.CostEstimate(flops=1, bytes_accessed=1, transcendentals=0),
        name=name,
        **more,
    )(*operands, *tokens)


def whole(shape):
    return pl.BlockSpec(shape, lambda *_: (0,) * len(shape))


def start_all(pairs, sems):
    copies = [
        pltpu.make_async_copy(src, dst, sems.at[at]) for at, (src, dst) in enumerate(pairs)
    ]
    for copy in copies:
        copy.start()
    return copies


def wait_all(copies):
    for copy in copies:
        copy.wait()


def place_of(inner):
    me = lax.axis_index("ctx")
    return lax.div(me, inner), lax.rem(me, inner)


def pack_cache_kernel(inner, *refs):
    sources, outs, made = refs[:4], refs[4 : 4 + OUTERS], refs[4 + OUTERS : 4 + 2 * OUTERS]
    cache, ids, weights, placement, sems, last = refs[4 + 2 * OUTERS :]
    copies = start_all(list(zip(sources, (cache, ids, weights, placement))), sems)
    outer, _ = place_of(inner)
    wait_all(copies[1:])
    keys = cache.shape[1]
    rows = ids.shape[1]
    experts = placement.shape[1]
    part = experts // OUTERS
    share = weights[...] / jnp.sum(weights[...], axis=0, keepdims=True)
    expert = lax.broadcasted_iota(jnp.int32, (experts, rows), 0)
    gates = jnp.zeros((experts, rows), F32)
    for k in range(ids.shape[0]):
        gates += jnp.where(ids[k : k + 1, :] == expert, share[k : k + 1, :], 0.0)
    high = gates.astype(BF16)
    low = (gates - high.astype(F32)).astype(BF16)
    place = lax.broadcasted_iota(jnp.int32, (2 * part, experts), 0)
    slot = jnp.broadcast_to(placement[...], (2 * part, experts))
    wait_all(copies[:1])
    sent = []
    for k in [1, 2, 3, 0]:
        to = outer ^ k
        block = made[k]
        column = pl.ds(pl.multiple_of(to * HEAD_SIZE, HEAD_SIZE), HEAD_SIZE)
        block[0:keys, :] = cache[0, :, column]
        block[keys : 2 * keys, :] = cache[1, :, column]
        first = to * part
        pick_high = jnp.where((slot == first + place) & (place < part), 1.0, 0.0).astype(BF16)
        pick_low = jnp.where((slot == first + place - part) & (place >= part), 1.0, 0.0)
        wanted = jnp.dot(pick_high, high, preferred_element_type=F32) + jnp.dot(
            pick_low.astype(BF16), low, preferred_element_type=F32
        )
        block[2 * keys :, :rows] = wanted.astype(BF16)
        block[2 * keys :, rows:] = jnp.zeros((2 * part, LANES - rows), BF16)
        copy = pltpu.make_async_copy(block, outs[k], last.at[k])
        copy.start()
        sent.append(copy)
    wait_all(sent)


def pack_queries_kernel(inner, *refs):
    sources, outs, made = refs[:2], refs[2 : 2 + OUTERS], refs[2 + OUTERS : 2 + 2 * OUTERS]
    queries, fresh, sems, last = refs[2 + 2 * OUTERS :]
    copies = start_all(list(zip(sources, (queries, fresh))), sems)
    outer, place = place_of(inner)
    rows = queries.shape[0]
    group = queries.shape[1] // (OUTERS * HEAD_SIZE)
    per_device = group // inner
    wait_all(copies)
    sent = []
    for k in [3, 2, 1, 0]:
        to = outer ^ k
        block = made[k]
        at = 0
        for h in range(group):
            head = to * group + (place ^ (h // per_device)) * per_device + h % per_device
            block[at : at + rows, :] = queries[
                :, pl.ds(pl.multiple_of(head * HEAD_SIZE, HEAD_SIZE), HEAD_SIZE)
            ]
            at += rows
        column = pl.ds(pl.multiple_of(to * HEAD_SIZE, HEAD_SIZE), HEAD_SIZE)
        block[at : at + rows, :] = fresh[0, :, column]
        block[at + rows :, :] = fresh[1, :, column]
        copy = pltpu.make_async_copy(block, outs[k], last.at[k])
        copy.start()
        sent.append(copy)
    wait_all(sent)


def merge_kernel(keys, *refs):
    blocks, out, sems = refs[:-2], refs[-2], refs[-1]
    gates = blocks[0].shape[0] - 2 * keys
    count = len(blocks)
    start = count * gates
    pairs = []
    for k in range(count):
        for at, size, to in (
            (2 * keys, gates, k * gates),
            (0, keys, start + k * keys),
            (keys, keys, start + (count + k) * keys),
        ):
            pairs.append((blocks[k].at[pl.ds(at, size)], out.at[pl.ds(to, size)]))
    wait_all(start_all(pairs, sems))


def attention_kernel(inner, group, rows, qf, *refs):
    caches, projections = refs[: 2 * inner], refs[2 * inner : 3 * inner]
    out, keys, values, attention = refs[3 * inner :]
    block = keys.shape[0] // (2 * inner)
    start = caches[0].shape[0] - 2 * block
    for j in range(2 * inner):
        keys[j * block : (j + 1) * block, :] = caches[j][start : start + block, :]
        values[j * block : (j + 1) * block, :] = caches[j][start + block :, :]
    factor = HEAD_SIZE ** (-0.5) * math.log2(math.e)
    own_key = qf[group * rows : (group + 1) * rows, :].astype(F32)
    own_value = qf[(group + 1) * rows :, :].astype(F32)
    step = max(1, group // 2)
    for h0 in range(0, group, step):
        query = qf[h0 * rows : (h0 + step) * rows, :]
        own = jnp.sum(
            query.astype(F32) * jnp.concatenate([own_key] * step, axis=0), axis=-1, keepdims=True
        )
        scores = lax.dot_general(query, keys[...], NT, preferred_element_type=F32)
        peak = jnp.maximum(own, jnp.max(scores, axis=-1, keepdims=True)) * factor
        weights = jnp.exp2(scores * factor - peak)
        own = jnp.exp2(own * factor - peak)
        totals = jnp.sum(weights, axis=-1, keepdims=True) + own
        weighted = jnp.dot(weights.astype(BF16), values[...], preferred_element_type=F32)
        weighted = weighted + own * jnp.concatenate([own_value] * step, axis=0)
        block_out = (weighted / totals).astype(BF16)
        for h in range(step):
            attention[:, (h0 + h) * HEAD_SIZE : (h0 + h + 1) * HEAD_SIZE] = block_out[
                h * rows : (h + 1) * rows, :
            ]
    depth = projections[0].shape[0]
    wide = math.gcd(out.shape[1], 512)
    for c in range(0, out.shape[1], wide):
        total = jnp.dot(
            attention[:, :depth], projections[0][:, c : c + wide], preferred_element_type=F32
        )
        for j in range(1, inner):
            total += jnp.dot(
                attention[:, j * depth : (j + 1) * depth],
                projections[j][:, c : c + wide],
                preferred_element_type=F32,
            )
        out[:, c : c + wide] = total.astype(out.dtype)


def select_kernel(inner, local, capacity, count, *refs):
    gates, (sel, selt, share) = refs[: 2 * inner], refs[2 * inner :]
    early = pl.program_id(0) < OUTERS // 2
    part = gates[0].shape[0] // 2
    spread = (
        lax.broadcasted_iota(jnp.int32, (2 * part, LANES), 0)
        == lax.broadcasted_iota(jnp.int32, (2 * part, LANES), 1)
    ).astype(F32)
    turn = (((0,), (0,)), ((), ()))
    pieces = []
    for j in halves(inner):
        block = jnp.where(early, gates[j][...], gates[inner + j][...])
        turned = lax.dot_general(block, spread.astype(BF16), turn, preferred_element_type=F32)
        pieces.append(turned.astype(BF16)[:count, :])
    table = jnp.concatenate(pieces, axis=0)
    rows = table.shape[0]
    first = place_of(inner)[1] * local
    lane = lax.broadcasted_iota(jnp.int32, (LANES, LANES), 1)
    sub = lax.broadcasted_iota(jnp.int32, (LANES, LANES), 0)
    pick = jnp.where((lane == first + sub) & (sub < local), 1.0, 0.0).astype(BF16)
    across = lax.dot_general(pick[:16], table, NT, preferred_element_type=F32)
    down = lax.dot_general(table, pick, NT, preferred_element_type=F32)
    r = lax.broadcasted_iota(jnp.int32, (rows, rows), 0)
    c = lax.broadcasted_iota(jnp.int32, (rows, rows), 1)
    upper = jnp.where(r <= c, 1.0, 0.0).astype(BF16)
    lower = jnp.where(c <= r, 1.0, 0.0).astype(BF16)
    across_rank = jnp.dot(
        jnp.where(across > 0, 1.0, 0.0).astype(BF16), upper, preferred_element_type=F32
    )
    across_rank = jnp.where(across > 0, across_rank, 0.0)
    down_rank = jnp.dot(
        lower, jnp.where(down > 0, 1.0, 0.0).astype(BF16), preferred_element_type=F32
    )
    down_rank = jnp.where(down > 0, down_rank, 0.0)
    place = lax.broadcasted_iota(jnp.int32, (capacity, rows), 0).astype(F32) + 1.0
    place_t = lax.broadcasted_iota(jnp.int32, (rows, capacity), 1).astype(F32) + 1.0
    column = lax.broadcasted_iota(jnp.int32, (capacity, LANES), 1)
    for e in range(local):
        chosen = jnp.where(across_rank[e : e + 1, :] == place, 1.0, 0.0).astype(BF16)
        sel[0, e * capacity : (e + 1) * capacity, :] = chosen
        selt[0, :, e * capacity : (e + 1) * capacity] = jnp.where(
            down_rank[:, e : e + 1] == place_t, 1.0, 0.0
        ).astype(BF16)
        mine = (column == first + e) | (column == first + e + part)
        found = jnp.dot(chosen, table, preferred_element_type=F32)
        value = jnp.sum(jnp.where(mine, found, 0.0), axis=-1, keepdims=True)
        share[0, e * capacity : (e + 1) * capacity, :] = jnp.broadcast_to(value, (capacity, LANES))


def norm_kernel(residual, gain, own, *refs):
    arrived, (hidden, normed) = refs[:-2], refs[-2:]
    total = own[...]
    for ref in arrived:
        total = total + ref[...].astype(F32)
    rounded = (residual[...].astype(F32) + total).astype(BF16)
    hidden[...] = rounded
    wide = rounded.astype(F32)
    scale = lax.rsqrt(jnp.mean(wide * wide, axis=-1, keepdims=True) + EPSILON)
    normed[...] = (wide * scale * gain[...]).astype(BF16)


def expert_kernel(inner, chunk, *refs):
    pieces = refs[:inner]
    sel, selt, share, gate_up, down = refs[inner : inner + 5]
    sel, selt, share = sel.at[chunk], selt.at[chunk], share.at[chunk]
    outs = refs[inner + 5 : 2 * inner + 5]
    stacked, packed, active, made = refs[2 * inner + 5 :]
    local, width, both = gate_up.shape
    ff = both // 2
    rows = pieces[0].shape[0]
    capacity = sel.shape[0] // local
    for at, j in enumerate(halves(inner)):
        stacked[at * rows : (at + 1) * rows, :] = pieces[j][...]
    wide = math.gcd(width, 512)
    tile = math.gcd(ff, 256)
    for c in range(0, width, wide):
        packed[:, c : c + wide] = jnp.dot(
            sel[...], stacked[:, c : c + wide], preferred_element_type=F32
        ).astype(BF16)
    for e in range(local):
        at = slice(e * capacity, (e + 1) * capacity)
        for f in range(0, ff, tile):
            left = jnp.dot(packed[at, :], gate_up[e, :, f : f + tile], preferred_element_type=F32)
            right = jnp.dot(
                packed[at, :], gate_up[e, :, ff + f : ff + f + tile], preferred_element_type=F32
            )
            active[at, f : f + tile] = (left / (1.0 + jnp.exp(-left)) * right).astype(BF16)
        for c in range(0, width, wide):
            produced = jnp.dot(active[at, :], down[e, :, c : c + wide], preferred_element_type=F32)
            made[at, c : c + wide] = (produced * share[at, 0:1]).astype(BF16)
    for c in range(0, width, wide):
        total = jnp.dot(selt[...], made[:, c : c + wide], preferred_element_type=F32).astype(BF16)
        for at, out in enumerate(outs):
            out[:, c : c + wide] = total[at * rows : (at + 1) * rows, :]


def hold_kernel(source, out, sem):
    copy = pltpu.make_async_copy(source, out, sem)
    copy.start()
    copy.wait()


def add_kernel(*refs):
    total = refs[0][...].astype(F32)
    for ref in refs[1:-1]:
        total = total + ref[...].astype(F32)
    refs[-1][...] = total.astype(refs[-1].dtype)


def local_program(
    n,
    queries,
    fresh,
    cache,
    residual,
    gain,
    out_proj,
    w_gate_up,
    w_down,
    route_ids,
    route_weights,
    placement,
):
    inner = n // OUTERS
    rows, width = residual.shape
    keys = cache.shape[1]
    group = queries.shape[1] // (OUTERS * HEAD_SIZE)
    local, _, both = w_gate_up.shape
    ff = both // 2
    experts_all = placement.shape[0]
    top = route_ids.shape[1]
    most = max(2, 3 * rows * top // (2 * experts_all))
    capacity = -(-most * inner // 16) * 16
    chunk_rows = rows * inner
    dma = pltpu.SemaphoreType.DMA
    ids_t, weights_t, slots = route_ids.T, route_weights.T, placement.reshape(1, -1)

    def pack(kernel, size, operands, name, tokens=()):
        return call(
            functools.partial(kernel, inner),
            [jax.ShapeDtypeStruct((size, HEAD_SIZE), BF16)] * OUTERS,
            operands,
            [ANY] * len(operands),
            name,
            tokens,
            limit=60,
            out_specs=[ANY] * OUTERS,
            scratch=[
                *[pltpu.VMEM((size, HEAD_SIZE), BF16)] * OUTERS,
                *[pltpu.VMEM(a.shape, a.dtype) for a in operands],
                dma((len(operands),)),
                dma((OUTERS,)),
            ],
        )

    gate_rows = 2 * experts_all // OUTERS
    cache_rows = 2 * keys + gate_rows
    packed = pack(
        pack_cache_kernel, cache_rows, (cache, ids_t, weights_t, slots), "pack_cache"
    )
    blocks = [packed[0]] + [swap(packed[k], n, k * inner) for k in range(1, OUTERS)]
    packed = pack(
        pack_queries_kernel, (group + 2) * rows, (queries, fresh), "pack_queries", (packed[0],)
    )
    asked = [packed[0]] + [swap(packed[k], n, k * inner) for k in range(1, OUTERS)]
    half_outers = OUTERS // 2
    caches, tokens = [], (packed[0],)
    for at in (0, half_outers):
        merged = call(
            functools.partial(merge_kernel, keys),
            jax.ShapeDtypeStruct((half_outers * cache_rows, HEAD_SIZE), BF16),
            blocks[at : at + half_outers],
            [ANY] * half_outers,
            "merge",
            tokens,
            out_specs=ANY,
            scratch=[dma((3 * half_outers,))],
        )
        caches += gather_inner(merged, n, *asked[1:])
        tokens = (merged,)
    projections = gather_inner(out_proj, n, caches[inner - 1], caches[-1])
    projections[0] = call(
        hold_kernel,
        jax.ShapeDtypeStruct(out_proj.shape, BF16),
        (out_proj,),
        [ANY],
        "hold",
        (merged,),
        out_specs=VMEM,
        scratch=[dma],
    )

    def add(terms, tokens=()):
        return call(
            add_kernel,
            jax.ShapeDtypeStruct((rows, width), BF16),
            terms,
            [VMEM] * len(terms),
            "add",
            tokens,
            out_specs=VMEM,
        )

    def attend(k, tokens, kind):
        return call(
            functools.partial(attention_kernel, inner, group, rows),
            jax.ShapeDtypeStruct((rows, width), kind),
            (asked[k], *caches, *projections),
            [VMEM] * (1 + 3 * inner),
            "attention",
            tokens,
            limit=18,
            out_specs=VMEM,
            scratch=[
                pltpu.VMEM((n * keys, HEAD_SIZE), BF16),
                pltpu.VMEM((n * keys, HEAD_SIZE), BF16),
                pltpu.VMEM((rows, group * HEAD_SIZE), BF16),
            ],
        )

    selected = [
        (local * capacity, chunk_rows),
        (chunk_rows, local * capacity),
        (local * capacity, LANES),
    ]
    kinds = [BF16, BF16, F32]
    last_half = half_outers - 1
    far = attend(3, (asked[1], asked[2]), BF16)
    across = attend(2, (far,), F32)
    near = attend(1, (across,), BF16)
    sent = add([across, swap(far, n, inner)], (near,))
    own = attend(0, (sent,), F32)
    home = [swap(near, n, inner), swap(sent, n, 2 * inner)]
    selection = call(
        functools.partial(select_kernel, inner, local, capacity, rows),
        [jax.ShapeDtypeStruct((OUTERS, *s), d) for s, d in zip(selected, kinds)],
        caches,
        [pl.BlockSpec((gate_rows, LANES), lambda k: (jnp.minimum(k, last_half), 0))] * inner
        + [pl.BlockSpec((gate_rows, LANES), lambda k: (jnp.maximum(k - half_outers, 0), 0))]
        * inner,
        "select",
        (own,),
        out_specs=[pl.BlockSpec((1, *s), lambda k: (k, 0, 0)) for s in selected],
        grid=(OUTERS,),
    )
    block = whole((rows, width))
    hidden, normed = call(
        norm_kernel,
        [jax.ShapeDtypeStruct((rows, width), BF16)] * 2,
        (residual, gain.reshape(1, -1), own, *home),
        [block, whole((1, width)), block, block, block],
        "norm",
        (selection[0],),
        out_specs=[block, block],
        grid=(1,),
    )

    def experts(k, pieces, tokens):
        return call(
            functools.partial(expert_kernel, inner, k),
            [jax.ShapeDtypeStruct((rows, width), BF16)] * inner,
            (*pieces, *selection, w_gate_up, w_down),
            [VMEM] * (inner + 5),
            "experts",
            tokens,
            limit=14,
            out_specs=[VMEM] * inner,
            scratch=[
                pltpu.VMEM((chunk_rows, width), BF16),
                pltpu.VMEM((local * capacity, width), BF16),
                pltpu.VMEM((local * capacity, ff), BF16),
                pltpu.VMEM((local * capacity, width), BF16),
            ],
        )

    bits = [1 << b for b in range(inner.bit_length() - 1)]
    first, second = swap(normed, n, inner), swap(normed, n, 2 * inner)
    around = gather_inner(normed, n)
    slots = [None] * OUTERS

    def fold(k):
        middle = len(slots[k]) // 2
        arrived = [swap(a, n, bits[0]) for a in slots[k][:middle - 1:-1]][::-1]
        slots[k] = [[a, b] for a, b in zip(slots[k][:middle], arrived)]

    def finish(k, tokens):
        terms = slots[k]
        for bit in bits[1:]:
            middle = len(terms) // 2
            sent = [add(t, tokens) for t in terms[middle:]]
            terms = [t + [swap(a, n, bit)] for t, a in zip(terms[:middle], sent)]
        return terms[0], sent[0]

    third = swap(second, n, inner)
    slots[0] = experts(0, around, ())
    fold(0)
    done = slots[0][0][0]
    slots[1] = experts(1, gather_inner(first, n, done), (done, second))
    fold(1)
    done = slots[1][0][0]
    slots[3] = experts(3, gather_inner(third, n, done), (done,))
    fold(3)
    done = slots[3][0][0]
    terms, sent = finish(3, (done,))
    slots[2] = experts(2, gather_inner(second, n, done), (sent,))
    fold(2)
    total = add(terms, (slots[2][0][0],))
    far = swap(total, n, inner)
    terms, sent = finish(2, (total,))
    total = add(terms + [far], (sent,))
    across = swap(total, n, 2 * inner)
    terms, sent = finish(1, (total,))
    total = add(terms, (sent,))
    near = swap(total, n, inner)
    terms, sent = finish(0, (total,))
    return hidden, add(terms + [near, across])


def solution(mesh):
    rows = P(("groups", "ctx"), None)
    middle = P(None, ("groups", "ctx"), None)
    in_specs = (
        rows,
        middle,
        middle,
        rows,
        P(),
        P("ctx", None),
        P("ctx", None, None),
        P("ctx", None, None),
        rows,
        rows,
        P(),
    )
    return jax.shard_map(
        functools.partial(local_program, mesh.shape["ctx"]),
        mesh=mesh,
        in_specs=in_specs,
        out_specs=(rows, rows),
        check_vma=False,
    )
```

```python
import functools
import math

import jax
import jax.numpy as jnp
from jax import lax
from jax.experimental import pallas as pl
from jax.experimental.pallas import tpu as pltpu
from jax.sharding import PartitionSpec as P

OUTERS = 4
HEAD_SIZE = 128
LANES = 128
EPSILON = 1e-06
MIB = 1 << 20
BF16, F32 = jnp.bfloat16, jnp.float32
PLAN = {
    "seq": ["E0", "E1", "E3", "f3", "E2", "t3", "f2", "t2", "f1", "t1", "f0"],
    "tok": {"E1": ["x2"]},
    "gate": {"c1": ["E0"], "c3": ["E1"], "c2": ["E3"]},
    "forward": True,
    "parts": 1,
    "cost": {"attention": 3000000000, "pack_queries": 6000000000, "norm": 6000000000},
    "mtok": ["pq"],
    "cgate": ["q1", "q2", "q3"],
    "pgate": ["cb"],
    "att": [3, 2, 1, "add", 0, "sel"],
    "atok": ["q1", "q2"],
}
NT = (((1,), (1,)), ((), ()))
ANY = pl.BlockSpec(memory_space=pl.ANY)
VMEM = pl.BlockSpec(memory_space=pltpu.VMEM)


def swap(array, n, offset):
    return lax.ppermute(array, "ctx", [(i, i ^ offset) for i in range(n)])


def after(array, *tokens):
    return lax.optimization_barrier((array, *tokens))[0]


def gather_inner(array, n, *tokens, far=None):
    pieces = {0: array}
    bit = n // OUTERS // 2
    if far is not None:
        pieces[bit] = far
    while bit:
        for j in list(pieces):
            if j | bit not in pieces:
                ready = after(pieces[j], *tokens) if j and tokens else pieces[j]
                pieces[j | bit] = swap(ready, n, bit)
        bit //= 2
    return [pieces[j] for j in range(n // OUTERS)]


def halves(inner):
    order, bit = [0], inner // 2
    while bit:
        order = order + [j | bit for j in order]
        bit //= 2
    return order


def call(kernel, outs, operands, specs, name, tokens=(), limit=16, scratch=(), out_specs=None, grid=None, cost=True):
    count = len(operands)

    def body(*refs):
        kernel(*refs[:count], *refs[count + len(tokens) :])

    more = {} if grid is None else {"grid": grid}
    return pl.pallas_call(
        body,
        out_shape=outs,
        in_specs=list(specs) + [ANY] * len(tokens),
        out_specs=out_specs,
        scratch_shapes=list(scratch),
        compiler_params=pltpu.CompilerParams(vmem_limit_bytes=limit * MIB),
        cost_estimate=pl.CostEstimate(flops=PLAN["cost"].get(name, 1), bytes_accessed=1, transcendentals=0),
        name=name,
        **more,
    )(*operands, *tokens)


def whole(shape):
    return pl.BlockSpec(shape, lambda *_: (0,) * len(shape))


def start_all(pairs, sems):
    copies = [
        pltpu.make_async_copy(src, dst, sems.at[at]) for at, (src, dst) in enumerate(pairs)
    ]
    for copy in copies:
        copy.start()
    return copies


def wait_all(copies):
    for copy in copies:
        copy.wait()


def place_of(inner):
    me = lax.axis_index("ctx")
    return lax.div(me, inner), lax.rem(me, inner)


def pack_cache_kernel(inner, *refs):
    sources, outs, made = refs[:4], refs[4 : 4 + OUTERS], refs[4 + OUTERS : 4 + 2 * OUTERS]
    cache, ids, weights, placement, sems, last = refs[4 + 2 * OUTERS :]
    copies = start_all(list(zip(sources, (cache, ids, weights, placement))), sems)
    outer, _ = place_of(inner)
    wait_all(copies[1:])
    keys = cache.shape[1]
    rows = ids.shape[1]
    experts = placement.shape[1]
    part = experts // OUTERS
    share = weights[...] / jnp.sum(weights[...], axis=0, keepdims=True)
    expert = lax.broadcasted_iota(jnp.int32, (experts, rows), 0)
    gates = jnp.zeros((experts, rows), F32)
    for k in range(ids.shape[0]):
        gates += jnp.where(ids[k : k + 1, :] == expert, share[k : k + 1, :], 0.0)
    high = gates.astype(BF16)
    low = (gates - high.astype(F32)).astype(BF16)
    place = lax.broadcasted_iota(jnp.int32, (2 * part, experts), 0)
    slot = jnp.broadcast_to(placement[...], (2 * part, experts))
    wait_all(copies[:1])
    sent = []
    for k in [1, 2, 3, 0]:
        to = outer ^ k
        block = made[k]
        column = pl.ds(pl.multiple_of(to * HEAD_SIZE, HEAD_SIZE), HEAD_SIZE)
        block[0:keys, :] = cache[0, :, column]
        block[keys : 2 * keys, :] = cache[1, :, column]
        first = to * part
        pick_high = jnp.where((slot == first + place) & (place < part), 1.0, 0.0).astype(BF16)
        pick_low = jnp.where((slot == first + place - part) & (place >= part), 1.0, 0.0)
        wanted = jnp.dot(pick_high, high, preferred_element_type=F32) + jnp.dot(
            pick_low.astype(BF16), low, preferred_element_type=F32
        )
        block[2 * keys :, :rows] = wanted.astype(BF16)
        block[2 * keys :, rows:] = jnp.zeros((2 * part, LANES - rows), BF16)
        copy = pltpu.make_async_copy(block, outs[k], last.at[k])
        copy.start()
        sent.append(copy)
    wait_all(sent)


def pack_queries_kernel(inner, *refs):
    sources, outs, made = refs[:2], refs[2 : 2 + OUTERS], refs[2 + OUTERS : 2 + 2 * OUTERS]
    queries, fresh, sems, last = refs[2 + 2 * OUTERS :]
    copies = start_all(list(zip(sources, (queries, fresh))), sems)
    outer, place = place_of(inner)
    rows = queries.shape[0]
    group = queries.shape[1] // (OUTERS * HEAD_SIZE)
    per_device = group // inner
    wait_all(copies)
    sent = []
    for k in [3, 2, 1, 0]:
        to = outer ^ k
        block = made[k]
        at = 0
        for h in range(group):
            head = to * group + (place ^ (h // per_device)) * per_device + h % per_device
            block[at : at + rows, :] = queries[
                :, pl.ds(pl.multiple_of(head * HEAD_SIZE, HEAD_SIZE), HEAD_SIZE)
            ]
            at += rows
        column = pl.ds(pl.multiple_of(to * HEAD_SIZE, HEAD_SIZE), HEAD_SIZE)
        block[at : at + rows, :] = fresh[0, :, column]
        block[at + rows :, :] = fresh[1, :, column]
        copy = pltpu.make_async_copy(block, outs[k], last.at[k])
        copy.start()
        sent.append(copy)
    wait_all(sent)


def merge_kernel(keys, *refs):
    blocks, out, sems = refs[:-2], refs[-2], refs[-1]
    gates = blocks[0].shape[0] - 2 * keys
    count = len(blocks)
    start = count * gates
    pairs = []
    for k in range(count):
        for at, size, to in (
            (2 * keys, gates, k * gates),
            (0, keys, start + k * keys),
            (keys, keys, start + (count + k) * keys),
        ):
            pairs.append((blocks[k].at[pl.ds(at, size)], out.at[pl.ds(to, size)]))
    wait_all(start_all(pairs, sems))


def attention_kernel(inner, group, rows, qf, *refs):
    caches, projections = refs[: 2 * inner], refs[2 * inner : 3 * inner]
    outs, (keys, values, attention) = refs[3 * inner : -3], refs[-3:]
    block = keys.shape[0] // (2 * inner)
    start = caches[0].shape[0] - 2 * block
    for j in range(2 * inner):
        keys[j * block : (j + 1) * block, :] = caches[j][start : start + block, :]
        values[j * block : (j + 1) * block, :] = caches[j][start + block :, :]
    factor = HEAD_SIZE ** (-0.5) * math.log2(math.e)
    own_key = qf[group * rows : (group + 1) * rows, :].astype(F32)
    own_value = qf[(group + 1) * rows :, :].astype(F32)
    step = max(1, group // 2)
    for h0 in range(0, group, step):
        query = qf[h0 * rows : (h0 + step) * rows, :]
        own = jnp.sum(
            query.astype(F32) * jnp.concatenate([own_key] * step, axis=0), axis=-1, keepdims=True
        )
        scores = lax.dot_general(query, keys[...], NT, preferred_element_type=F32)
        peak = jnp.maximum(own, jnp.max(scores, axis=-1, keepdims=True)) * factor
        weights = jnp.exp2(scores * factor - peak)
        own = jnp.exp2(own * factor - peak)
        totals = jnp.sum(weights, axis=-1, keepdims=True) + own
        weighted = jnp.dot(weights.astype(BF16), values[...], preferred_element_type=F32)
        weighted = weighted + own * jnp.concatenate([own_value] * step, axis=0)
        block_out = (weighted / totals).astype(BF16)
        for h in range(step):
            attention[:, (h0 + h) * HEAD_SIZE : (h0 + h + 1) * HEAD_SIZE] = block_out[
                h * rows : (h + 1) * rows, :
            ]
    depth = projections[0].shape[0]
    columns = outs[0].shape[1]
    wide = math.gcd(columns, 512)
    for c in range(0, columns * len(outs), wide):
        total = jnp.dot(
            attention[:, :depth], projections[0][:, c : c + wide], preferred_element_type=F32
        )
        for j in range(1, inner):
            total += jnp.dot(
                attention[:, j * depth : (j + 1) * depth],
                projections[j][:, c : c + wide],
                preferred_element_type=F32,
            )
        out = outs[c // columns]
        out[:, c % columns : c % columns + wide] = total.astype(out.dtype)


def select_kernel(inner, local, capacity, count, *refs):
    gates, (sel, selt, share) = refs[: 2 * inner], refs[2 * inner :]
    early = pl.program_id(0) < OUTERS // 2
    part = gates[0].shape[0] // 2
    spread = (
        lax.broadcasted_iota(jnp.int32, (2 * part, LANES), 0)
        == lax.broadcasted_iota(jnp.int32, (2 * part, LANES), 1)
    ).astype(F32)
    turn = (((0,), (0,)), ((), ()))
    pieces = []
    for j in halves(inner):
        block = jnp.where(early, gates[j][...], gates[inner + j][...])
        turned = lax.dot_general(block, spread.astype(BF16), turn, preferred_element_type=F32)
        pieces.append(turned.astype(BF16)[:count, :])
    table = jnp.concatenate(pieces, axis=0)
    rows = table.shape[0]
    first = place_of(inner)[1] * local
    lane = lax.broadcasted_iota(jnp.int32, (LANES, LANES), 1)
    sub = lax.broadcasted_iota(jnp.int32, (LANES, LANES), 0)
    pick = jnp.where((lane == first + sub) & (sub < local), 1.0, 0.0).astype(BF16)
    across = lax.dot_general(pick[:16], table, NT, preferred_element_type=F32)
    down = lax.dot_general(table, pick, NT, preferred_element_type=F32)
    r = lax.broadcasted_iota(jnp.int32, (rows, rows), 0)
    c = lax.broadcasted_iota(jnp.int32, (rows, rows), 1)
    upper = jnp.where(r <= c, 1.0, 0.0).astype(BF16)
    lower = jnp.where(c <= r, 1.0, 0.0).astype(BF16)
    across_rank = jnp.dot(
        jnp.where(across > 0, 1.0, 0.0).astype(BF16), upper, preferred_element_type=F32
    )
    across_rank = jnp.where(across > 0, across_rank, 0.0)
    down_rank = jnp.dot(
        lower, jnp.where(down > 0, 1.0, 0.0).astype(BF16), preferred_element_type=F32
    )
    down_rank = jnp.where(down > 0, down_rank, 0.0)
    place = lax.broadcasted_iota(jnp.int32, (capacity, rows), 0).astype(F32) + 1.0
    place_t = lax.broadcasted_iota(jnp.int32, (rows, capacity), 1).astype(F32) + 1.0
    column = lax.broadcasted_iota(jnp.int32, (capacity, LANES), 1)
    for e in range(local):
        chosen = jnp.where(across_rank[e : e + 1, :] == place, 1.0, 0.0).astype(BF16)
        sel[0, e * capacity : (e + 1) * capacity, :] = chosen
        selt[0, :, e * capacity : (e + 1) * capacity] = jnp.where(
            down_rank[:, e : e + 1] == place_t, 1.0, 0.0
        ).astype(BF16)
        mine = (column == first + e) | (column == first + e + part)
        found = jnp.dot(chosen, table, preferred_element_type=F32)
        value = jnp.sum(jnp.where(mine, found, 0.0), axis=-1, keepdims=True)
        share[0, e * capacity : (e + 1) * capacity, :] = jnp.broadcast_to(value, (capacity, LANES))


def norm_kernel(count, residual, gain, *refs):
    arrived, narrow, (hidden, normed) = refs[: -2 - count], refs[-2 - count : -2], refs[-2:]
    total = jnp.concatenate([ref[...].astype(F32) for ref in narrow], axis=1)
    for ref in arrived:
        total = total + ref[...].astype(F32)
    rounded = (residual[...].astype(F32) + total).astype(BF16)
    hidden[...] = rounded
    wide = rounded.astype(F32)
    scale = lax.rsqrt(jnp.mean(wide * wide, axis=-1, keepdims=True) + EPSILON)
    normed[...] = (wide * scale * gain[...]).astype(BF16)


def expert_kernel(inner, chunk, *refs):
    pieces = refs[:inner]
    sel, selt, share, gate_up, down = refs[inner : inner + 5]
    sel, selt, share = sel.at[chunk], selt.at[chunk], share.at[chunk]
    outs = refs[inner + 5 : 2 * inner + 5]
    stacked, packed, active, made = refs[2 * inner + 5 :]
    local, width, both = gate_up.shape
    ff = both // 2
    rows = pieces[0].shape[0]
    capacity = sel.shape[0] // local
    for at, j in enumerate(halves(inner)):
        stacked[at * rows : (at + 1) * rows, :] = pieces[j][...]
    wide = math.gcd(width, 512)
    tile = math.gcd(ff, 256)
    for c in range(0, width, wide):
        packed[:, c : c + wide] = jnp.dot(
            sel[...], stacked[:, c : c + wide], preferred_element_type=F32
        ).astype(BF16)
    for e in range(local):
        at = slice(e * capacity, (e + 1) * capacity)
        for f in range(0, ff, tile):
            left = jnp.dot(packed[at, :], gate_up[e, :, f : f + tile], preferred_element_type=F32)
            right = jnp.dot(
                packed[at, :], gate_up[e, :, ff + f : ff + f + tile], preferred_element_type=F32
            )
            active[at, f : f + tile] = (left / (1.0 + jnp.exp(-left)) * right).astype(BF16)
        for c in range(0, width, wide):
            produced = jnp.dot(active[at, :], down[e, :, c : c + wide], preferred_element_type=F32)
            made[at, c : c + wide] = (produced * share[at, 0:1]).astype(BF16)
    for c in range(0, width, wide):
        total = jnp.dot(selt[...], made[:, c : c + wide], preferred_element_type=F32).astype(BF16)
        for at, out in enumerate(outs):
            out[:, c : c + wide] = total[at * rows : (at + 1) * rows, :]


def add_kernel(at, *refs):
    out = refs[-1]
    wide = out.shape[1]
    total = jnp.zeros(out.shape, F32)
    for ref in refs[:-1]:
        total = total + (ref[:, at : at + wide] if ref.shape[1] > wide else ref[...]).astype(F32)
    out[...] = total.astype(out.dtype)


def gather_columns_kernel(count, *refs):
    out, narrow = refs[-1], refs[-1 - count : -1]
    wide = narrow[0].shape[1]
    for p in range(count):
        at = slice(p * wide, (p + 1) * wide)
        total = narrow[p][...].astype(F32)
        for ref in refs[: -1 - count]:
            total = total + ref[:, at].astype(F32)
        out[:, at] = total.astype(out.dtype)


def local_program(
    n,
    queries,
    fresh,
    cache,
    residual,
    gain,
    out_proj,
    w_gate_up,
    w_down,
    route_ids,
    route_weights,
    placement,
):
    inner = n // OUTERS
    rows, width = residual.shape
    keys = cache.shape[1]
    group = queries.shape[1] // (OUTERS * HEAD_SIZE)
    local, _, both = w_gate_up.shape
    ff = both // 2
    experts_all = placement.shape[0]
    top = route_ids.shape[1]
    most = max(2, 3 * rows * top // (2 * experts_all))
    capacity = -(-most * inner // 16) * 16
    chunk_rows = rows * inner
    dma = pltpu.SemaphoreType.DMA
    ids_t, weights_t, slots = route_ids.T, route_weights.T, placement.reshape(1, -1)

    def pack(kernel, size, operands, name, tokens=()):
        return call(
            functools.partial(kernel, inner),
            [jax.ShapeDtypeStruct((size, HEAD_SIZE), BF16)] * OUTERS,
            operands,
            [ANY] * len(operands),
            name,
            tokens,
            limit=60,
            out_specs=[ANY] * OUTERS,
            scratch=[
                *[pltpu.VMEM((size, HEAD_SIZE), BF16)] * OUTERS,
                *[pltpu.VMEM(a.shape, a.dtype) for a in operands],
                dma((len(operands),)),
                dma((OUTERS,)),
            ],
        )

    gate_rows = 2 * experts_all // OUTERS
    cache_rows = 2 * keys + gate_rows
    packed = pack(
        pack_cache_kernel, cache_rows, (cache, ids_t, weights_t, slots), "pack_cache"
    )
    blocks = [packed[0]] + [swap(packed[k], n, k * inner) for k in range(1, OUTERS)]
    packed = pack(
        pack_queries_kernel, (group + 2) * rows, (queries, fresh), "pack_queries", (packed[0],)
    )
    asked = [packed[0]] + [swap(packed[k], n, k * inner) for k in range(1, OUTERS)]
    half_outers, half = OUTERS // 2, inner // 2
    front = {"pq": packed[0], "q1": asked[1], "q2": asked[2], "q3": asked[3]}
    caches, tokens = [], [front[t] for t in PLAN["mtok"]]
    for at, name in ((0, "a"), (half_outers, "b")):
        merged = call(
            functools.partial(merge_kernel, keys),
            jax.ShapeDtypeStruct((half_outers * cache_rows, HEAD_SIZE), BF16),
            blocks[at : at + half_outers],
            [ANY] * half_outers,
            "merge",
            tokens,
            out_specs=ANY,
            scratch=[dma((3 * half_outers,))],
        )
        caches += gather_inner(merged, n, *[front[t] for t in PLAN["cgate"]])
        tokens = (merged,)
        front["m" + name], front["y" + name], front["c" + name] = merged, caches[half - inner], caches[-1]
    projections = gather_inner(out_proj, n, *[front[t] for t in PLAN["pgate"]])

    parts = PLAN["parts"]
    columns = width // parts

    def add(terms, tokens=(), part=None):
        return call(
            functools.partial(add_kernel, 0 if part is None else part * columns),
            jax.ShapeDtypeStruct((rows, width if part is None else columns), BF16),
            terms,
            [VMEM] * len(terms),
            "add",
            tokens,
            out_specs=VMEM,
        )

    def add_parts(terms, others, tokens):
        done = []
        for p in range(parts):
            done.append(add(terms + [t[p] for t in others], tokens, p))
            tokens = (done[-1],)
        return done

    def attend(k, tokens, kind, pieces=1):
        return call(
            functools.partial(attention_kernel, inner, group, rows),
            [jax.ShapeDtypeStruct((rows, width // pieces), kind)] * pieces,
            (asked[k], *caches, *projections),
            [VMEM] * (1 + 3 * inner),
            "attention",
            tokens,
            limit=18,
            out_specs=[VMEM] * pieces,
            scratch=[
                pltpu.VMEM((n * keys, HEAD_SIZE), BF16),
                pltpu.VMEM((n * keys, HEAD_SIZE), BF16),
                pltpu.VMEM((rows, group * HEAD_SIZE), BF16),
            ],
        )

    selected = [
        (local * capacity, chunk_rows),
        (chunk_rows, local * capacity),
        (local * capacity, LANES),
    ]
    kinds = [BF16, BF16, F32]
    last_half = half_outers - 1
    def select(tokens):
        return call(
            functools.partial(select_kernel, inner, local, capacity, rows),
            [jax.ShapeDtypeStruct((OUTERS, *s), d) for s, d in zip(selected, kinds)],
            caches,
            [pl.BlockSpec((gate_rows, LANES), lambda k: (jnp.minimum(k, last_half), 0))] * inner
            + [pl.BlockSpec((gate_rows, LANES), lambda k: (jnp.maximum(k - half_outers, 0), 0))]
            * inner,
            "select",
            tokens,
            out_specs=[pl.BlockSpec((1, *s), lambda k: (k, 0, 0)) for s in selected],
            grid=(OUTERS,),
        )

    parts_done, tokens = {}, [front[t] for t in PLAN["atok"]]
    for step in PLAN["att"]:
        if step == "sel":
            selection = select(tokens)
            tokens = (selection[0],)
            continue
        if step == "add":
            parts_done[step] = add_parts(parts_done[2], [far], tokens)
        else:
            kind, pieces = (F32 if step in (0, 2) else BF16), (parts if step == 3 else 1)
            parts_done[step] = list(attend(step, tokens, kind, pieces))
        tokens = (parts_done[step][-1],)
        if step == 3:
            far = [swap(a, n, inner) for a in parts_done[3]]
    own, near = parts_done[0][0], swap(parts_done[1][0], n, inner)
    home = [swap(a, n, 2 * inner) for a in parts_done["add"]]
    block = whole((rows, width))
    hidden, normed = call(
        functools.partial(norm_kernel, parts),
        [jax.ShapeDtypeStruct((rows, width), BF16)] * 2,
        (residual, gain.reshape(1, -1), own, near, *home),
        [block, whole((1, width)), block, block] + [whole((rows, columns))] * parts,
        "norm",
        tokens,
        out_specs=[block, block],
        grid=(1,),
    )

    def experts(k, pieces, tokens):
        return call(
            functools.partial(expert_kernel, inner, k),
            [jax.ShapeDtypeStruct((rows, width), BF16)] * inner,
            (*pieces, *selection, w_gate_up, w_down),
            [VMEM] * (inner + 5),
            "experts",
            tokens,
            limit=14,
            out_specs=[VMEM] * inner,
            scratch=[
                pltpu.VMEM((chunk_rows, width), BF16),
                pltpu.VMEM((local * capacity, width), BF16),
                pltpu.VMEM((local * capacity, ff), BF16),
                pltpu.VMEM((local * capacity, width), BF16),
            ],
        )

    bits = [1 << b for b in range(inner.bit_length() - 1)]
    made = {"x0": normed, "x1": swap(normed, n, inner), "x2": swap(normed, n, 2 * inner)}

    def waiting(array, name):
        gates = PLAN["gate"].get(name, ())
        return after(array, *[get(t) for t in gates]) if gates else array

    def fold(slots):
        middle = len(slots) // 2
        arrived = [swap(a, n, bits[0]) for a in slots[: middle - 1 : -1]][::-1]
        return [[a, b] for a, b in zip(slots[:middle], arrived)]

    def get(name):
        if name not in made:
            made[name] = make(name[0], int(name[1]), name)
        return made[name]

    def make(kind, k, name):
        if name == "x3":
            return swap(waiting(get("x2"), name), n, inner)
        if kind == "y":
            return swap(waiting(get("x%d" % k), name), n, half)
        at = PLAN["seq"].index(name)
        tokens = [get(t) for t in PLAN["seq"][max(at - 1, 0) : at] + PLAN["tok"].get(name, [])]
        if kind == "E":
            gates = [get(t) for t in PLAN["gate"].get("c%d" % k, ())]
            outs = experts(k, gather_inner(get("x%d" % k), n, *gates, far=get("y%d" % k)), tokens)
            made["slots%d" % k] = fold(outs)
            return outs[0]
        if kind == "f":
            get("E%d" % k)
            terms = made["slots%d" % k]
            for bit in bits[1:]:
                middle = len(terms) // 2
                sent = [add(t, tokens) for t in terms[middle:]]
                terms = [t + [swap(a, n, bit)] for t, a in zip(terms[:middle], sent)]
            made["terms%d" % k] = terms[0]
            return sent[0]
        get("f%d" % k)
        terms = made["terms%d" % k]
        if not PLAN["forward"] or k == 1:
            return add(terms, tokens)
        if k == 2:
            get("t3")
        made["sums%d" % k] = add_parts(terms, [made["far"]] if k == 2 else [], tokens)
        if k == 3:
            made["far"] = [swap(a, n, inner) for a in made["sums3"]]
        return made["sums%d" % k][-1]

    for name in PLAN["seq"]:
        get(name)
    near = swap(made["t1"], n, inner)
    if not PLAN["forward"]:
        arrivals = [near, swap(made["t2"], n, 2 * inner), swap(made["t3"], n, 3 * inner)]
        return hidden, add(made["terms0"] + arrivals)
    across = [swap(a, n, 2 * inner) for a in made["sums2"]]
    total = call(
        functools.partial(gather_columns_kernel, parts),
        jax.ShapeDtypeStruct((rows, width), BF16),
        made["terms0"] + [near] + across,
        [VMEM] * (len(made["terms0"]) + 1 + parts),
        "add",
        out_specs=VMEM,
    )
    return hidden, total


def solution(mesh):
    rows = P(("groups", "ctx"), None)
    middle = P(None, ("groups", "ctx"), None)
    in_specs = (
        rows,
        middle,
        middle,
        rows,
        P(),
        P("ctx", None),
        P("ctx", None, None),
        P("ctx", None, None),
        rows,
        rows,
        P(),
    )
    return jax.shard_map(
        functools.partial(local_program, mesh.shape["ctx"]),
        mesh=mesh,
        in_specs=in_specs,
        out_specs=(rows, rows),
        check_vma=False,
    )
```

```python
import functools
import math

import jax
import jax.numpy as jnp
from jax import lax
from jax.experimental import pallas as pl
from jax.experimental.pallas import tpu as pltpu
from jax.sharding import PartitionSpec as P

OUTERS = 4
HEAD_SIZE = 128
LANES = 128
EPSILON = 1e-06
MIB = 1 << 20
BF16, F32 = jnp.bfloat16, jnp.float32
PLAN = {
    "seq": ["E0", "E1", "E3", "f3", "E2", "t3", "f2", "t2", "f1", "t1", "f0"],
    "tok": {"E1": ["x2"]},
    "gate": {"c1": ["E0"], "c3": ["E1"], "c2": ["E3"]},
    "forward": True,
    "parts": 1,
    "cost": {"attention": 3000000000, "pack_queries": 6000000000, "norm": 6000000000},
    "mtok": ["pq"],
    "cgate": ["q1", "q2", "q3"],
    "pgate": ["cb"],
    "att": [3, 1, 2, "add", 0, "sel"],
    "atok": ["q2"],
}
NT = (((1,), (1,)), ((), ()))
ANY = pl.BlockSpec(memory_space=pl.ANY)
VMEM = pl.BlockSpec(memory_space=pltpu.VMEM)


def swap(array, n, offset):
    return lax.ppermute(array, "ctx", [(i, i ^ offset) for i in range(n)])


def after(array, *tokens):
    return lax.optimization_barrier((array, *tokens))[0]


def gather_inner(array, n, *tokens, far=None):
    pieces = {0: array}
    bit = n // OUTERS // 2
    if far is not None:
        pieces[bit] = far
    while bit:
        for j in list(pieces):
            if j | bit not in pieces:
                ready = after(pieces[j], *tokens) if j and tokens else pieces[j]
                pieces[j | bit] = swap(ready, n, bit)
        bit //= 2
    return [pieces[j] for j in range(n // OUTERS)]


def halves(inner):
    order, bit = [0], inner // 2
    while bit:
        order = order + [j | bit for j in order]
        bit //= 2
    return order


def call(kernel, outs, operands, specs, name, tokens=(), limit=16, scratch=(), out_specs=None, grid=None, cost=True):
    count = len(operands)

    def body(*refs):
        kernel(*refs[:count], *refs[count + len(tokens) :])

    more = {} if grid is None else {"grid": grid}
    return pl.pallas_call(
        body,
        out_shape=outs,
        in_specs=list(specs) + [ANY] * len(tokens),
        out_specs=out_specs,
        scratch_shapes=list(scratch),
        compiler_params=pltpu.CompilerParams(vmem_limit_bytes=limit * MIB),
        cost_estimate=pl.CostEstimate(flops=PLAN["cost"].get(name, 1), bytes_accessed=1, transcendentals=0),
        name=name,
        **more,
    )(*operands, *tokens)


def whole(shape):
    return pl.BlockSpec(shape, lambda *_: (0,) * len(shape))


def start_all(pairs, sems):
    copies = [
        pltpu.make_async_copy(src, dst, sems.at[at]) for at, (src, dst) in enumerate(pairs)
    ]
    for copy in copies:
        copy.start()
    return copies


def wait_all(copies):
    for copy in copies:
        copy.wait()


def place_of(inner):
    me = lax.axis_index("ctx")
    return lax.div(me, inner), lax.rem(me, inner)


def pack_cache_kernel(inner, *refs):
    sources, outs, made = refs[:4], refs[4 : 4 + OUTERS], refs[4 + OUTERS : 4 + 2 * OUTERS]
    cache, ids, weights, placement, sems, last = refs[4 + 2 * OUTERS :]
    copies = start_all(list(zip(sources, (cache, ids, weights, placement))), sems)
    outer, _ = place_of(inner)
    wait_all(copies[1:])
    keys = cache.shape[1]
    rows = ids.shape[1]
    experts = placement.shape[1]
    part = experts // OUTERS
    share = weights[...] / jnp.sum(weights[...], axis=0, keepdims=True)
    expert = lax.broadcasted_iota(jnp.int32, (experts, rows), 0)
    gates = jnp.zeros((experts, rows), F32)
    for k in range(ids.shape[0]):
        gates += jnp.where(ids[k : k + 1, :] == expert, share[k : k + 1, :], 0.0)
    high = gates.astype(BF16)
    low = (gates - high.astype(F32)).astype(BF16)
    place = lax.broadcasted_iota(jnp.int32, (2 * part, experts), 0)
    slot = jnp.broadcast_to(placement[...], (2 * part, experts))
    wait_all(copies[:1])
    sent = []
    for k in [1, 2, 3, 0]:
        to = outer ^ k
        block = made[k]
        column = pl.ds(pl.multiple_of(to * HEAD_SIZE, HEAD_SIZE), HEAD_SIZE)
        block[0:keys, :] = cache[0, :, column]
        block[keys : 2 * keys, :] = cache[1, :, column]
        first = to * part
        pick_high = jnp.where((slot == first + place) & (place < part), 1.0, 0.0).astype(BF16)
        pick_low = jnp.where((slot == first + place - part) & (place >= part), 1.0, 0.0)
        wanted = jnp.dot(pick_high, high, preferred_element_type=F32) + jnp.dot(
            pick_low.astype(BF16), low, preferred_element_type=F32
        )
        block[2 * keys :, :rows] = wanted.astype(BF16)
        block[2 * keys :, rows:] = jnp.zeros((2 * part, LANES - rows), BF16)
        copy = pltpu.make_async_copy(block, outs[k], last.at[k])
        copy.start()
        sent.append(copy)
    wait_all(sent)


def pack_queries_kernel(inner, *refs):
    sources, outs, made = refs[:2], refs[2 : 2 + OUTERS], refs[2 + OUTERS : 2 + 2 * OUTERS]
    queries, fresh, sems, last = refs[2 + 2 * OUTERS :]
    copies = start_all(list(zip(sources, (queries, fresh))), sems)
    outer, place = place_of(inner)
    rows = queries.shape[0]
    group = queries.shape[1] // (OUTERS * HEAD_SIZE)
    per_device = group // inner
    wait_all(copies)
    sent = []
    for k in [3, 2, 1, 0]:
        to = outer ^ k
        block = made[k]
        at = 0
        for h in range(group):
            head = to * group + (place ^ (h // per_device)) * per_device + h % per_device
            block[at : at + rows, :] = queries[
                :, pl.ds(pl.multiple_of(head * HEAD_SIZE, HEAD_SIZE), HEAD_SIZE)
            ]
            at += rows
        column = pl.ds(pl.multiple_of(to * HEAD_SIZE, HEAD_SIZE), HEAD_SIZE)
        block[at : at + rows, :] = fresh[0, :, column]
        block[at + rows :, :] = fresh[1, :, column]
        copy = pltpu.make_async_copy(block, outs[k], last.at[k])
        copy.start()
        sent.append(copy)
    wait_all(sent)


def merge_kernel(keys, *refs):
    blocks, out, sems = refs[:-2], refs[-2], refs[-1]
    gates = blocks[0].shape[0] - 2 * keys
    count = len(blocks)
    start = count * gates
    pairs = []
    for k in range(count):
        for at, size, to in (
            (2 * keys, gates, k * gates),
            (0, keys, start + k * keys),
            (keys, keys, start + (count + k) * keys),
        ):
            pairs.append((blocks[k].at[pl.ds(at, size)], out.at[pl.ds(to, size)]))
    wait_all(start_all(pairs, sems))


def attention_kernel(inner, group, rows, qf, *refs):
    caches, projections = refs[: 2 * inner], refs[2 * inner : 3 * inner]
    outs, (keys, values, attention) = refs[3 * inner : -3], refs[-3:]
    block = keys.shape[0] // (2 * inner)
    start = caches[0].shape[0] - 2 * block
    for j in range(2 * inner):
        keys[j * block : (j + 1) * block, :] = caches[j][start : start + block, :]
        values[j * block : (j + 1) * block, :] = caches[j][start + block :, :]
    factor = HEAD_SIZE ** (-0.5) * math.log2(math.e)
    own_key = qf[group * rows : (group + 1) * rows, :].astype(F32)
    own_value = qf[(group + 1) * rows :, :].astype(F32)
    step = max(1, group // 4)
    for h0 in range(0, group, step):
        query = qf[h0 * rows : (h0 + step) * rows, :]
        own = jnp.sum(
            query.astype(F32) * jnp.concatenate([own_key] * step, axis=0), axis=-1, keepdims=True
        )
        scores = lax.dot_general(query, keys[...], NT, preferred_element_type=F32)
        peak = jnp.maximum(own, jnp.max(scores, axis=-1, keepdims=True)) * factor
        weights = jnp.exp2(scores * factor - peak)
        own = jnp.exp2(own * factor - peak)
        totals = jnp.sum(weights, axis=-1, keepdims=True) + own
        weighted = jnp.dot(weights.astype(BF16), values[...], preferred_element_type=F32)
        weighted = weighted + own * jnp.concatenate([own_value] * step, axis=0)
        block_out = (weighted / totals).astype(BF16)
        for h in range(step):
            attention[:, (h0 + h) * HEAD_SIZE : (h0 + h + 1) * HEAD_SIZE] = block_out[
                h * rows : (h + 1) * rows, :
            ]
    depth = projections[0].shape[0]
    columns = outs[0].shape[1]
    wide = math.gcd(columns, 512)
    for c in range(0, columns * len(outs), wide):
        total = jnp.dot(
            attention[:, :depth], projections[0][:, c : c + wide], preferred_element_type=F32
        )
        for j in range(1, inner):
            total += jnp.dot(
                attention[:, j * depth : (j + 1) * depth],
                projections[j][:, c : c + wide],
                preferred_element_type=F32,
            )
        out = outs[c // columns]
        out[:, c % columns : c % columns + wide] = total.astype(out.dtype)


def select_kernel(inner, local, capacity, count, *refs):
    gates, (sel, selt, share) = refs[: 2 * inner], refs[2 * inner :]
    early = pl.program_id(0) < OUTERS // 2
    part = gates[0].shape[0] // 2
    spread = (
        lax.broadcasted_iota(jnp.int32, (2 * part, LANES), 0)
        == lax.broadcasted_iota(jnp.int32, (2 * part, LANES), 1)
    ).astype(F32)
    turn = (((0,), (0,)), ((), ()))
    pieces = []
    for j in halves(inner):
        block = jnp.where(early, gates[j][...], gates[inner + j][...])
        turned = lax.dot_general(block, spread.astype(BF16), turn, preferred_element_type=F32)
        pieces.append(turned.astype(BF16)[:count, :])
    table = jnp.concatenate(pieces, axis=0)
    rows = table.shape[0]
    first = place_of(inner)[1] * local
    lane = lax.broadcasted_iota(jnp.int32, (LANES, LANES), 1)
    sub = lax.broadcasted_iota(jnp.int32, (LANES, LANES), 0)
    pick = jnp.where((lane == first + sub) & (sub < local), 1.0, 0.0).astype(BF16)
    across = lax.dot_general(pick[:16], table, NT, preferred_element_type=F32)
    down = lax.dot_general(table, pick, NT, preferred_element_type=F32)
    r = lax.broadcasted_iota(jnp.int32, (rows, rows), 0)
    c = lax.broadcasted_iota(jnp.int32, (rows, rows), 1)
    upper = jnp.where(r <= c, 1.0, 0.0).astype(BF16)
    lower = jnp.where(c <= r, 1.0, 0.0).astype(BF16)
    across_rank = jnp.dot(
        jnp.where(across > 0, 1.0, 0.0).astype(BF16), upper, preferred_element_type=F32
    )
    across_rank = jnp.where(across > 0, across_rank, 0.0)
    down_rank = jnp.dot(
        lower, jnp.where(down > 0, 1.0, 0.0).astype(BF16), preferred_element_type=F32
    )
    down_rank = jnp.where(down > 0, down_rank, 0.0)
    place = lax.broadcasted_iota(jnp.int32, (capacity, rows), 0).astype(F32) + 1.0
    place_t = lax.broadcasted_iota(jnp.int32, (rows, capacity), 1).astype(F32) + 1.0
    column = lax.broadcasted_iota(jnp.int32, (capacity, LANES), 1)
    for e in range(local):
        chosen = jnp.where(across_rank[e : e + 1, :] == place, 1.0, 0.0).astype(BF16)
        sel[0, e * capacity : (e + 1) * capacity, :] = chosen
        selt[0, :, e * capacity : (e + 1) * capacity] = jnp.where(
            down_rank[:, e : e + 1] == place_t, 1.0, 0.0
        ).astype(BF16)
        mine = (column == first + e) | (column == first + e + part)
        found = jnp.dot(chosen, table, preferred_element_type=F32)
        value = jnp.sum(jnp.where(mine, found, 0.0), axis=-1, keepdims=True)
        share[0, e * capacity : (e + 1) * capacity, :] = jnp.broadcast_to(value, (capacity, LANES))


def norm_kernel(count, residual, gain, *refs):
    arrived, narrow, (hidden, normed) = refs[: -2 - count], refs[-2 - count : -2], refs[-2:]
    total = jnp.concatenate([ref[...].astype(F32) for ref in narrow], axis=1)
    for ref in arrived:
        total = total + ref[...].astype(F32)
    rounded = (residual[...].astype(F32) + total).astype(BF16)
    hidden[...] = rounded
    wide = rounded.astype(F32)
    scale = lax.rsqrt(jnp.mean(wide * wide, axis=-1, keepdims=True) + EPSILON)
    normed[...] = (wide * scale * gain[...]).astype(BF16)


def expert_kernel(inner, chunk, *refs):
    pieces = refs[:inner]
    sel, selt, share, gate_up, down = refs[inner : inner + 5]
    sel, selt, share = sel.at[chunk], selt.at[chunk], share.at[chunk]
    outs = refs[inner + 5 : 2 * inner + 5]
    stacked, packed, active, made = refs[2 * inner + 5 :]
    local, width, both = gate_up.shape
    ff = both // 2
    rows = pieces[0].shape[0]
    capacity = sel.shape[0] // local
    for at, j in enumerate(halves(inner)):
        stacked[at * rows : (at + 1) * rows, :] = pieces[j][...]
    wide = math.gcd(width, 512)
    tile = math.gcd(ff, 256)
    for c in range(0, width, wide):
        packed[:, c : c + wide] = jnp.dot(
            sel[...], stacked[:, c : c + wide], preferred_element_type=F32
        ).astype(BF16)
    for e in range(local):
        at = slice(e * capacity, (e + 1) * capacity)
        for f in range(0, ff, tile):
            left = jnp.dot(packed[at, :], gate_up[e, :, f : f + tile], preferred_element_type=F32)
            right = jnp.dot(
                packed[at, :], gate_up[e, :, ff + f : ff + f + tile], preferred_element_type=F32
            )
            active[at, f : f + tile] = (left / (1.0 + jnp.exp(-left)) * right).astype(BF16)
        for c in range(0, width, wide):
            produced = jnp.dot(active[at, :], down[e, :, c : c + wide], preferred_element_type=F32)
            made[at, c : c + wide] = (produced * share[at, 0:1]).astype(BF16)
    for c in range(0, width, wide):
        total = jnp.dot(selt[...], made[:, c : c + wide], preferred_element_type=F32).astype(BF16)
        for at, out in enumerate(outs):
            out[:, c : c + wide] = total[at * rows : (at + 1) * rows, :]


def add_kernel(at, *refs):
    out = refs[-1]
    wide = out.shape[1]
    total = jnp.zeros(out.shape, F32)
    for ref in refs[:-1]:
        total = total + (ref[:, at : at + wide] if ref.shape[1] > wide else ref[...]).astype(F32)
    out[...] = total.astype(out.dtype)


def gather_columns_kernel(count, *refs):
    out, narrow = refs[-1], refs[-1 - count : -1]
    wide = narrow[0].shape[1]
    for p in range(count):
        at = slice(p * wide, (p + 1) * wide)
        total = narrow[p][...].astype(F32)
        for ref in refs[: -1 - count]:
            total = total + ref[:, at].astype(F32)
        out[:, at] = total.astype(out.dtype)


def local_program(
    n,
    queries,
    fresh,
    cache,
    residual,
    gain,
    out_proj,
    w_gate_up,
    w_down,
    route_ids,
    route_weights,
    placement,
):
    inner = n // OUTERS
    rows, width = residual.shape
    keys = cache.shape[1]
    group = queries.shape[1] // (OUTERS * HEAD_SIZE)
    local, _, both = w_gate_up.shape
    ff = both // 2
    experts_all = placement.shape[0]
    top = route_ids.shape[1]
    most = max(2, 3 * rows * top // (2 * experts_all))
    capacity = -(-most * inner // 16) * 16
    chunk_rows = rows * inner
    dma = pltpu.SemaphoreType.DMA
    ids_t, weights_t, slots = route_ids.T, route_weights.T, placement.reshape(1, -1)

    def pack(kernel, size, operands, name, tokens=()):
        return call(
            functools.partial(kernel, inner),
            [jax.ShapeDtypeStruct((size, HEAD_SIZE), BF16)] * OUTERS,
            operands,
            [ANY] * len(operands),
            name,
            tokens,
            limit=60,
            out_specs=[ANY] * OUTERS,
            scratch=[
                *[pltpu.VMEM((size, HEAD_SIZE), BF16)] * OUTERS,
                *[pltpu.VMEM(a.shape, a.dtype) for a in operands],
                dma((len(operands),)),
                dma((OUTERS,)),
            ],
        )

    gate_rows = 2 * experts_all // OUTERS
    cache_rows = 2 * keys + gate_rows
    packed = pack(
        pack_cache_kernel, cache_rows, (cache, ids_t, weights_t, slots), "pack_cache"
    )
    blocks = [packed[0]] + [swap(packed[k], n, k * inner) for k in range(1, OUTERS)]
    packed = pack(
        pack_queries_kernel, (group + 2) * rows, (queries, fresh), "pack_queries", (packed[0],)
    )
    asked = [packed[0]] + [swap(packed[k], n, k * inner) for k in range(1, OUTERS)]
    half_outers, half = OUTERS // 2, inner // 2
    front = {"pq": packed[0], "q1": asked[1], "q2": asked[2], "q3": asked[3]}
    caches, tokens = [], [front[t] for t in PLAN["mtok"]]
    for at, name in ((0, "a"), (half_outers, "b")):
        merged = call(
            functools.partial(merge_kernel, keys),
            jax.ShapeDtypeStruct((half_outers * cache_rows, HEAD_SIZE), BF16),
            blocks[at : at + half_outers],
            [ANY] * half_outers,
            "merge",
            tokens,
            out_specs=ANY,
            scratch=[dma((3 * half_outers,))],
        )
        caches += gather_inner(merged, n, *[front[t] for t in PLAN["cgate"]])
        tokens = (merged,)
        front["m" + name], front["y" + name], front["c" + name] = merged, caches[half - inner], caches[-1]
    projections = gather_inner(out_proj, n, *[front[t] for t in PLAN["pgate"]])

    parts = PLAN["parts"]
    columns = width // parts

    def add(terms, tokens=(), part=None):
        return call(
            functools.partial(add_kernel, 0 if part is None else part * columns),
            jax.ShapeDtypeStruct((rows, width if part is None else columns), BF16),
            terms,
            [VMEM] * len(terms),
            "add",
            tokens,
            out_specs=VMEM,
        )

    def add_parts(terms, others, tokens):
        done = []
        for p in range(parts):
            done.append(add(terms + [t[p] for t in others], tokens, p))
            tokens = (done[-1],)
        return done

    def attend(k, tokens, kind, pieces=1):
        return call(
            functools.partial(attention_kernel, inner, group, rows),
            [jax.ShapeDtypeStruct((rows, width // pieces), kind)] * pieces,
            (asked[k], *caches, *projections),
            [VMEM] * (1 + 3 * inner),
            "attention",
            tokens,
            limit=18,
            out_specs=[VMEM] * pieces,
            scratch=[
                pltpu.VMEM((n * keys, HEAD_SIZE), BF16),
                pltpu.VMEM((n * keys, HEAD_SIZE), BF16),
                pltpu.VMEM((rows, group * HEAD_SIZE), BF16),
            ],
        )

    selected = [
        (local * capacity, chunk_rows),
        (chunk_rows, local * capacity),
        (local * capacity, LANES),
    ]
    kinds = [BF16, BF16, F32]
    last_half = half_outers - 1
    def select(tokens):
        return call(
            functools.partial(select_kernel, inner, local, capacity, rows),
            [jax.ShapeDtypeStruct((OUTERS, *s), d) for s, d in zip(selected, kinds)],
            caches,
            [pl.BlockSpec((gate_rows, LANES), lambda k: (jnp.minimum(k, last_half), 0))] * inner
            + [pl.BlockSpec((gate_rows, LANES), lambda k: (jnp.maximum(k - half_outers, 0), 0))]
            * inner,
            "select",
            tokens,
            out_specs=[pl.BlockSpec((1, *s), lambda k: (k, 0, 0)) for s in selected],
            grid=(OUTERS,),
        )

    parts_done, tokens = {}, [front[t] for t in PLAN["atok"]]
    for step in PLAN["att"]:
        if step == "sel":
            selection = select(tokens)
            tokens = (selection[0],)
            continue
        if step == "add":
            parts_done[step] = add_parts(parts_done[2], [far], tokens)
        else:
            kind, pieces = (F32 if step in (0, 2) else BF16), (parts if step == 3 else 1)
            parts_done[step] = list(attend(step, tokens, kind, pieces))
        tokens = (parts_done[step][-1],)
        if step == 3:
            far = [swap(a, n, inner) for a in parts_done[3]]
    own, near = parts_done[0][0], swap(parts_done[1][0], n, inner)
    home = [swap(a, n, 2 * inner) for a in parts_done["add"]]
    block = whole((rows, width))
    hidden, normed = call(
        functools.partial(norm_kernel, parts),
        [jax.ShapeDtypeStruct((rows, width), BF16)] * 2,
        (residual, gain.reshape(1, -1), own, near, *home),
        [block, whole((1, width)), block, block] + [whole((rows, columns))] * parts,
        "norm",
        tokens,
        out_specs=[block, block],
        grid=(1,),
    )

    def experts(k, pieces, tokens):
        return call(
            functools.partial(expert_kernel, inner, k),
            [jax.ShapeDtypeStruct((rows, width), BF16)] * inner,
            (*pieces, *selection, w_gate_up, w_down),
            [VMEM] * (inner + 5),
            "experts",
            tokens,
            limit=14,
            out_specs=[VMEM] * inner,
            scratch=[
                pltpu.VMEM((chunk_rows, width), BF16),
                pltpu.VMEM((local * capacity, width), BF16),
                pltpu.VMEM((local * capacity, ff), BF16),
                pltpu.VMEM((local * capacity, width), BF16),
            ],
        )

    bits = [1 << b for b in range(inner.bit_length() - 1)]
    made = {"x0": normed, "x1": swap(normed, n, inner), "x2": swap(normed, n, 2 * inner)}

    def waiting(array, name):
        gates = PLAN["gate"].get(name, ())
        return after(array, *[get(t) for t in gates]) if gates else array

    def fold(slots):
        middle = len(slots) // 2
        arrived = [swap(a, n, bits[0]) for a in slots[: middle - 1 : -1]][::-1]
        return [[a, b] for a, b in zip(slots[:middle], arrived)]

    def get(name):
        if name not in made:
            made[name] = make(name[0], int(name[1]), name)
        return made[name]

    def make(kind, k, name):
        if name == "x3":
            return swap(waiting(get("x2"), name), n, inner)
        if kind == "y":
            return swap(waiting(get("x%d" % k), name), n, half)
        at = PLAN["seq"].index(name)
        tokens = [get(t) for t in PLAN["seq"][max(at - 1, 0) : at] + PLAN["tok"].get(name, [])]
        if kind == "E":
            gates = [get(t) for t in PLAN["gate"].get("c%d" % k, ())]
            outs = experts(k, gather_inner(get("x%d" % k), n, *gates, far=get("y%d" % k)), tokens)
            made["slots%d" % k] = fold(outs)
            return outs[0]
        if kind == "f":
            get("E%d" % k)
            terms = made["slots%d" % k]
            for bit in bits[1:]:
                middle = len(terms) // 2
                sent = [add(t, tokens) for t in terms[middle:]]
                terms = [t + [swap(a, n, bit)] for t, a in zip(terms[:middle], sent)]
            made["terms%d" % k] = terms[0]
            return sent[0]
        get("f%d" % k)
        terms = made["terms%d" % k]
        if not PLAN["forward"] or k == 1:
            return add(terms, tokens)
        if k == 2:
            get("t3")
        made["sums%d" % k] = add_parts(terms, [made["far"]] if k == 2 else [], tokens)
        if k == 3:
            made["far"] = [swap(a, n, inner) for a in made["sums3"]]
        return made["sums%d" % k][-1]

    for name in PLAN["seq"]:
        get(name)
    near = swap(made["t1"], n, inner)
    if not PLAN["forward"]:
        arrivals = [near, swap(made["t2"], n, 2 * inner), swap(made["t3"], n, 3 * inner)]
        return hidden, add(made["terms0"] + arrivals)
    across = [swap(a, n, 2 * inner) for a in made["sums2"]]
    total = call(
        functools.partial(gather_columns_kernel, parts),
        jax.ShapeDtypeStruct((rows, width), BF16),
        made["terms0"] + [near] + across,
        [VMEM] * (len(made["terms0"]) + 1 + parts),
        "add",
        out_specs=VMEM,
    )
    return hidden, total


def solution(mesh):
    rows = P(("groups", "ctx"), None)
    middle = P(None, ("groups", "ctx"), None)
    in_specs = (
        rows,
        middle,
        middle,
        rows,
        P(),
        P("ctx", None),
        P("ctx", None, None),
        P("ctx", None, None),
        rows,
        rows,
        P(),
    )
    return jax.shard_map(
        functools.partial(local_program, mesh.shape["ctx"]),
        mesh=mesh,
        in_specs=in_specs,
        out_specs=(rows, rows),
        check_vma=False,
    )
```
